512 devices in a mesh: seq: 32 (over y, x, core), head: 16 (over z).
Axes of the slice: x: 4, y: 4, z: 16, core: 2. Of those that a mesh axis runs over, the one named last changes fastest.
Arguments:
- queries: bfloat16 [8192, 4096], P('seq', 'head'), may hold values from -6 to 6
- keys: bfloat16 [8192, 4096], P('seq', 'head'), may hold values from -6 to 6
- values: bfloat16 [8192, 4096], P('seq', 'head'), may hold values from -6 to 6
- gate: bfloat16 [8192, 4096], P('seq', 'head'), may hold values from -6 to 6
- log_forget: float32 [32, 8192], P('head', 'seq'), may hold values from -1.5 to 0
- write_rate: float32 [32, 8192], P('head', 'seq'), may hold values from 0 to 1
- level_weight: float32 [32, 8, 8192], P('head', None, 'seq'), may hold values from 0.25 to 2.5
- w_out: bfloat16 [4096, 4096], P('head'), may hold values from -0.09375 to 0.09375
Outputs:
- mixed: bfloat16 [8192, 4096], P(('seq', 'head'))
The draws below stay inside these ranges and needn't reach their ends.
All inputs are finite; a program needn't handle non-finite values.
Results may differ from the reference program's by a relative error of at most 0.02.
Values may be sent and summed in bfloat16 or wider, within the bound.
No kernel may reach another device: no remote copies, remote signals or barrier semaphores. Data moves between devices by JAX's collectives and lax.ppermute only.
A program may use at most 64 MiB of HBM per device.

```python
import math
import jax
import jax.numpy as jnp
from jax import lax

D = 4096
DK = 128
HEAD_DEV = 2
BLOCK = 64
TOK_DEV = 256
HEADS = 32
TOKENS = 8192
LEVELS = 8
N_HEAD = 16


def draw_log_forget(key, part):
    streams = jax.random.split(key, 5)
    slowest = 0.1 / TOKENS
    fastest = 1.0 / 40.0
    spread = jax.random.uniform(streams[0], (HEADS, 1), jnp.float32)
    update_speeds = jnp.exp(jnp.log(slowest) + spread * (jnp.log(fastest) - jnp.log(slowest)))
    slabs = TOKENS // TOK_DEV
    section_factor = jnp.exp(jax.random.uniform(streams[1], (HEADS, slabs), jnp.float32, -0.6931, 0.6931))
    section_factor = jnp.repeat(section_factor, TOK_DEV, axis=1)
    approximate_guess = jax.random.uniform(streams[2], (HEADS, TOKENS), jnp.float32, 0.5, 1.5)
    chosen_locations = jax.random.randint(streams[3], (2,), 0, TOKENS)
    fading_falls = jax.random.uniform(streams[4], (2,), jnp.float32, -0.6931, -0.2231)
    item_indices = jnp.arange(TOKENS)
    sudden_jumps = jnp.where(item_indices == chosen_locations[0], fading_falls[0], 0.0) + jnp.where(item_indices == chosen_locations[1], fading_falls[1], 0.0)
    return -(update_speeds * section_factor * approximate_guess) + sudden_jumps[None, :]


def draw_write_rate(key, part):
    streams = jax.random.split(jax.random.fold_in(key, 17), 3)
    centers = jax.random.uniform(streams[0], (HEADS, 1), jnp.float32, -6.0, 1.0)
    noise = 0.75 * jax.random.normal(streams[2], (HEADS, TOKENS), jnp.float32)
    return jax.nn.sigmoid(centers + noise).astype(jnp.float32)


def block_scale(own_key, shape, shards, smallest, high):
    factor_of = 1.0
    for position, blocks in shards:
        heights = jax.random.uniform(jax.random.fold_in(jax.random.fold_in(own_key, 6), position), (blocks,), jnp.float32, smallest / len(shards), high / len(shards))
        factor_of = factor_of * jnp.repeat(jnp.exp(heights), shape[position] // blocks).reshape((-1,) + (1,) * (len(shape) - 1 - position))
    return factor_of


def scatter_about(key, extent, scale, reach, cuts=(), kind=jnp.bfloat16):
    values = jax.random.normal(key, extent, jnp.float32) * scale
    if len(cuts) > 0:
        values = block_scale(key, extent, cuts, -0.22, 0.18) * values
    return jnp.clip(values, min=-reach, max=reach).astype(kind)


def setup_inputs(seed: int = 0) -> dict:
    streams_of = jax.random.split(jax.random.key(seed), 9)
    return {
        "queries": scatter_about(streams_of[0], (TOKENS, HEADS * DK), 1.0, 6.0, ((0, 32), (1, 16))),
        "keys": scatter_about(streams_of[1], (TOKENS, HEADS * DK), 1.0, 6.0, ((0, 32), (1, 16))),
        "values": scatter_about(streams_of[2], (TOKENS, HEADS * DK), 1.0, 6.0, ((0, 32), (1, 16))),
        "gate": scatter_about(streams_of[3], (TOKENS, HEADS * DK), 1.0, 6.0, ((0, 32), (1, 16))),
        "log_forget": draw_log_forget(jax.random.fold_in(streams_of[8], 71), 0),
        "write_rate": draw_write_rate(jax.random.fold_in(streams_of[8], 71), 0),
        "level_weight": jnp.clip(jnp.exp(math.log(2.5) - 2.3025851 * jax.random.uniform(streams_of[6], (HEADS, LEVELS, TOKENS), jnp.float32) ** block_scale(streams_of[6], (HEADS, LEVELS, TOKENS), ((0, 16), (2, 32)), -0.2, 0.2)), 0.25, 2.5),
        "w_out": scatter_about(streams_of[7], (HEADS * DK, D), (HEADS * DK) ** -0.5, 0.09375, ((0, 16),)),
    }


EPSILON = 1e-06
PRECISE = lax.Precision.HIGHEST

def unit_rows(matrix):
    floated = matrix.astype(jnp.float32)
    return floated * lax.rsqrt(lax.optimization_barrier(jnp.sum(floated * floated, axis=-1, keepdims=True)) + EPSILON)

def token_step(carried, inputs):
    memory, product = carried
    query_row, key_row, value_row, retain, strength = inputs
    prod_key = jnp.einsum('hij,hj->hi', product, key_row, precision=PRECISE)
    product = retain[:, None, None] * (product - strength[:, None, None] * prod_key[:, :, None] * key_row[:, None, :])
    mem_key = jnp.einsum('hij,hj->hi', memory, key_row, precision=PRECISE)
    memory = retain[:, None, None] * (memory - strength[:, None, None] * mem_key[:, :, None] * key_row[:, None, :])
    memory = memory + strength[:, None, None] * value_row[:, :, None] * key_row[:, None, :]
    reach_row = jnp.einsum('hij,hj->hi', product, query_row, precision=PRECISE)
    own_row = jnp.einsum('hij,hj->hi', memory, query_row, precision=PRECISE)
    return ((memory, product), (reach_row, own_row))

def reference(queries, keys, values, gate, log_forget, write_rate, level_weight, w_out):
    groups = TOKENS // BLOCK
    level_count = LEVELS - 1
    query_rows = unit_rows(queries.reshape(TOKENS, HEADS, DK)).reshape(groups, BLOCK, HEADS, DK)
    key_rows = unit_rows(keys.reshape(TOKENS, HEADS, DK)).reshape(groups, BLOCK, HEADS, DK)
    value_rows = values.astype(jnp.float32).reshape(groups, BLOCK, HEADS, DK)
    retain = jnp.exp(log_forget).T.reshape(groups, BLOCK, HEADS)
    strength = write_rate.T.reshape(groups, BLOCK, HEADS)
    weights = jnp.transpose(level_weight, (2, 0, 1)).reshape(groups, BLOCK, HEADS, LEVELS)
    level_axis = jnp.arange(level_count, dtype=jnp.int32)
    identity = jnp.broadcast_to(jnp.eye(DK, dtype=jnp.float32), (HEADS, DK, DK))

    def block_step(stored, inputs):
        block_queries, block_keys, block_values, block_retain, block_strength, block_weights, ordinal = inputs
        start = (jnp.zeros((HEADS, DK, DK), jnp.float32), identity)
        (ending, moving), (reach_rows, own_rows) = lax.scan(token_step, start, (block_queries, block_keys, block_values, block_retain, block_strength))
        level_reads = jnp.einsum('hlvk,chk->chlv', stored, reach_rows, precision=PRECISE)
        core_rows = block_weights[:, :, 0, None] * own_rows
        core_rows = core_rows + jnp.einsum('chl,chlv->chv', block_weights[:, :, 1:], level_reads, precision=PRECISE)
        merge_level = jnp.int32(0)
        for exponent in range(1, level_count + 1):
            merge_level = merge_level + ((ordinal + 1) % 2 ** exponent == 0).astype(jnp.int32)
        below_mask = (level_axis < merge_level)[None, :, None, None]
        equal_mask = (level_axis == merge_level)[None, :, None, None]
        above_mask = (level_axis > merge_level)[None, :, None, None]
        merged = lax.optimization_barrier(jnp.sum(jnp.where(below_mask, stored, 0.0), axis=1, keepdims=True))
        carried = jnp.where(above_mask, stored, jnp.where(equal_mask, merged, 0.0))
        carried = jnp.einsum('hlij,hjk->hlik', carried, moving, precision=PRECISE)
        carried = carried + jnp.where(equal_mask, ending[:, None], 0.0)
        return (carried, core_rows)
    initial = jnp.zeros((HEADS, level_count, DK, DK), jnp.float32)
    ordinals = jnp.arange(groups, dtype=jnp.int32)
    _, cores = lax.scan(block_step, initial, (query_rows, key_rows, value_rows, retain, strength, weights, ordinals))
    cores = cores.reshape(TOKENS, HEADS, DK)
    scaled = cores * lax.rsqrt(lax.optimization_barrier(jnp.mean(cores * cores, axis=-1, keepdims=True)) + EPSILON)
    gated = scaled * jax.nn.silu(gate.astype(jnp.float32).reshape(TOKENS, HEADS, DK))
    normed = gated.reshape(TOKENS, HEADS * DK).astype(jnp.bfloat16)
    group_width = HEAD_DEV * DK
    pieces = jnp.transpose(normed.reshape(TOKENS, N_HEAD, group_width), (1, 0, 2))
    group_weights = w_out.reshape(N_HEAD, group_width, D)

    def add_group(running, inputs):
        group_rows, group_matrix = inputs
        partial_value = jnp.dot(group_rows, group_matrix, preferred_element_type=jnp.float32).astype(jnp.bfloat16)
        return (running + partial_value.astype(jnp.float32), None)
    running, _ = lax.scan(add_group, jnp.zeros((TOKENS, D), jnp.float32), (pieces, group_weights))
    return running.astype(jnp.bfloat16)
```

```python
import jax
import jax.numpy as jnp
from jax import lax
from jax.experimental import pallas as pl
from jax.experimental.pallas import tpu as pltpu
from jax.sharding import PartitionSpec as P

DK = 128
BLOCK = 64
EPSILON = 1e-06
F32 = jnp.float32
BF16 = jnp.bfloat16
VMEM = pl.BlockSpec(memory_space=pltpu.VMEM)
SMEM = pl.BlockSpec(memory_space=pltpu.SMEM)
VMEM_BYTES = 48 * 1024 * 1024


def dot(left, right, dims=((1,), (0,)), precision=None):
    return lax.dot_general(left, right, (dims, ((), ())), precision=precision, preferred_element_type=F32)


def halves(matrix):
    high = matrix.astype(BF16)
    return high, (matrix - high.astype(F32)).astype(BF16)


def dot3(left, right):
    (lh, ll), (rh, rl) = left, right
    return dot(lh, rh) + (dot(lh, rl) + dot(ll, rh))


def dot2(left, right):
    high, low = halves(left)
    return dot(high, right) + dot(low, right)


def block_masks(tokens):
    row = lax.broadcasted_iota(jnp.int32, (tokens, tokens), 0)
    col = lax.broadcasted_iota(jnp.int32, (tokens, tokens), 1)
    same = row // BLOCK == col // BLOCK
    return row, col, same


def states_kernel(k_ref, v_ref, lf_ref, wr_ref, x_ref, y_ref, w_ref, u_ref, rows_ref):
    tokens = k_ref.shape[0]
    heads = lf_ref.shape[0]
    blocks = tokens // BLOCK
    row, col, same = block_masks(tokens)
    inclusive = same & (row >= col)
    strict = same & (row > col)
    eye = (row == col).astype(F32)
    log_forget = lf_ref[...]
    rate = wr_ref[...]
    exact = lax.Precision.HIGHEST
    cum = dot(log_forget, inclusive.astype(F32), ((1,), (1,)), exact)
    total = dot(log_forget, same.astype(F32), ((1,), (1,)), exact)
    pad = jnp.zeros((8 - 3 * heads, tokens), F32)
    columns = jnp.concatenate([cum, total, rate, pad], axis=0).T
    eye_state = (
        lax.broadcasted_iota(jnp.int32, (DK, DK), 0) == lax.broadcasted_iota(jnp.int32, (DK, DK), 1)
    ).astype(F32)
    inv_key_rows = []
    lowers, keys, norms = [], [], []
    for h in range(heads):
        key = k_ref[:, h * DK : (h + 1) * DK]
        key_f = key.astype(F32)
        key_key = dot(key, key, ((1,), (1,)))
        inv_col = lax.rsqrt(jnp.sum(key_f * key_f, axis=1, keepdims=True) + EPSILON)
        inv_row = lax.rsqrt(jnp.sum(key_key * eye, axis=0, keepdims=True) + EPSILON)
        inv_key_rows.append(inv_row)
        rate_col = columns[:, 2 * heads + h : 2 * heads + h + 1]
        lowers.append(jnp.where(strict, key_key * (rate_col * inv_col) * inv_row, 0.0))
        keys.append((key, key_f))
        norms.append((inv_col, inv_row))
    inverses = [eye - jnp.where(row // 2 == col // 2, lower, 0.0) for lower in lowers]
    width = 2
    while width < BLOCK:
        band = (row // width != col // width) & (row // (2 * width) == col // (2 * width))
        nexts = []
        for h in range(heads):
            inverse = halves(inverses[h])
            inner = dot3(halves(jnp.where(band, lowers[h], 0.0)), inverse)
            nexts.append(inverses[h] - dot3(inverse, halves(inner)))
        inverses = nexts
        width *= 2
    for h in range(heads):
        key, key_f = keys[h]
        inv_col, inv_row = norms[h]
        value = v_ref[:, h * DK : (h + 1) * DK]
        cum_row = cum[h : h + 1]
        cum_col = columns[:, h : h + 1]
        total_col = columns[:, heads + h : heads + h + 1]
        rate_row = rate[h : h + 1]
        fading = jnp.exp(jnp.where(inclusive, cum_col - cum_row, -1e30))
        solved = inverses[h] * rate_row
        bases = dot2(solved * inv_row, key)
        writes = dot2(solved * fading, value)
        w_ref[:, h * DK : (h + 1) * DK] = bases
        u_ref[:, h * DK : (h + 1) * DK] = writes
        both = jnp.concatenate(
            [writes * (jnp.exp(total_col - cum_col) * inv_col), bases * inv_col], axis=1
        )
        both_high, both_low = halves(both)
        leaf = []
        for g in range(blocks):
            span = slice(g * BLOCK, (g + 1) * BLOCK)
            turned = key_f[span].T.astype(BF16)
            raw = dot(turned, both_high[span]) + dot(turned, both_low[span])
            fade = jnp.exp(total[h : h + 1, g * BLOCK : g * BLOCK + 1])
            leaf.append(jnp.concatenate([raw[:, :DK], fade * (eye_state - raw[:, DK:])], axis=1))
        short = [x.astype(BF16) for x in leaf]

        def merge(lead, trail):
            moved = dot(trail[:, DK:].astype(BF16), lead.astype(BF16))
            return jnp.concatenate([moved[:, :DK] + trail[:, :DK], moved[:, DK:]], axis=1)

        first = merge(leaf[0], leaf[1])
        second = merge(leaf[2], leaf[3])
        y_ref[h, 0] = short[0]
        y_ref[h, 1] = first.astype(BF16)
        y_ref[h, 2] = dot(short[2][:, DK:], first.astype(BF16)).astype(BF16)
        y_ref[h, 3] = short[2]
        x_ref[h] = merge(first, second).astype(BF16)
    rows_ref[...] = jnp.concatenate([cum] + inv_key_rows + [jnp.zeros((8 - 2 * heads, tokens), F32)], axis=0)


def reads_kernel(q_ref, k_ref, w_ref, u_ref, rows_ref, y_ref, lw_ref, core_ref, lift_ref):
    tokens = k_ref.shape[0]
    heads = y_ref.shape[0]
    row, col, same = block_masks(tokens)
    inclusive = same & (row >= col)
    rows = rows_ref[...]
    columns = rows.T
    levels = lw_ref.shape[1]
    weights = lw_ref[...].reshape(heads * levels, tokens).T
    for h in range(heads):
        lanes = slice(h * DK, (h + 1) * DK)
        query = q_ref[:, lanes]
        key = k_ref[:, lanes]
        query_f = query.astype(F32)
        inv_query = lax.rsqrt(jnp.sum(query_f * query_f, axis=1, keepdims=True) + EPSILON)
        query_key = dot(query, key, ((1,), (1,))) * inv_query * rows[heads + h : heads + h + 1]
        cum_col = columns[:, h : h + 1]
        fading = jnp.exp(jnp.where(inclusive, cum_col - rows[h : h + 1], -1e30))
        own = dot3(halves(query_key * fading), halves(u_ref[:, lanes]))
        masked = jnp.where(inclusive, query_key, 0.0)
        reach = jnp.exp(cum_col) * (query_f * inv_query - dot3(halves(masked), halves(w_ref[:, lanes])))
        reach_s = reach.astype(BF16)

        def weight(level, span):
            at = h * levels + level
            return weights[span, at : at + 1]

        spans = [slice(g * BLOCK, (g + 1) * BLOCK) for g in range(4)]
        read1 = dot(reach_s[spans[1]], y_ref[h, 0])
        read2 = dot(reach_s[spans[2]], y_ref[h, 1])
        read3 = dot(reach_s[spans[3]], y_ref[h, 2])
        near3 = dot(reach_s[spans[3]], y_ref[h, 3, :, :DK])
        core_ref[spans[0], lanes] = weight(0, spans[0]) * own[spans[0]]
        core_ref[spans[1], lanes] = weight(0, spans[1]) * own[spans[1]] + weight(1, spans[1]) * read1[:, :DK]
        core_ref[spans[2], lanes] = weight(0, spans[2]) * own[spans[2]] + weight(2, spans[2]) * read2[:, :DK]
        core_ref[spans[3], lanes] = (
            weight(0, spans[3]) * own[spans[3]]
            + weight(1, spans[3]) * near3
            + weight(2, spans[3]) * read3[:, :DK]
        )
        lift_ref[spans[0], lanes] = reach_s[spans[0]]
        lift_ref[spans[1], lanes] = read1[:, DK:].astype(BF16)
        lift_ref[spans[2], lanes] = read2[:, DK:].astype(BF16)
        lift_ref[spans[3], lanes] = read3[:, DK:].astype(BF16)


def merge_kernel(bit, pos_ref, mine_ref, theirs_ref, before_ref, total_ref, level_ref, after_ref):
    upper = (pos_ref[0] >> bit) & 1 == 1
    heads = mine_ref.shape[0]

    def joined(lead, trail):
        moved = dot(trail[:, DK:], lead)
        return jnp.concatenate([moved[:, :DK] + trail[:, :DK].astype(F32), moved[:, DK:]], axis=1).astype(BF16)

    @pl.when(upper)
    def _():
        for h in range(heads):
            total_ref[h] = joined(theirs_ref[h], mine_ref[h])
        for h in range(heads):
            if bit == 0:
                level_ref[h] = theirs_ref[h, :, :DK]
                after_ref[h] = theirs_ref[h, :, DK:]
            else:
                read = dot(before_ref[h], theirs_ref[h]).astype(BF16)
                level_ref[h] = read[:, :DK]
                after_ref[h] = read[:, DK:]

    @pl.when(jnp.logical_not(upper))
    def _():
        for h in range(heads):
            total_ref[h] = joined(mine_ref[h], theirs_ref[h])
        level_ref[...] = jnp.zeros(level_ref.shape, level_ref.dtype)
        after_ref[...] = before_ref[...]


def final_kernel(outer, ring, pos_ref, core_ref, lift_ref, last_ref, before_ref, lw_ref, gate_ref, out_w_ref, *rest):
    level_refs, out_ref, norm_ref, turn_ref = rest[:-3], rest[-3], rest[-2], rest[-1]
    heads = before_ref.shape[0]
    tokens = core_ref.shape[0]
    levels = lw_ref.shape[1]
    weights = lw_ref[...].reshape(heads * levels, tokens).T
    upper = ((pos_ref[0] >> (outer - 1)) & 1 == 1).astype(F32)
    normed = []
    for h in range(heads):
        lanes = slice(h * DK, (h + 1) * DK)
        lifted = lift_ref[:, lanes].astype(F32)
        last = (dot(before_ref[h], last_ref[h]) * upper).astype(BF16)
        scaled, stack = [], []
        for b in range(outer):
            at = h * levels + levels - outer + b
            scaled.append((lifted * weights[:, at : at + 1]).astype(BF16))
            stack.append(level_refs[b][h] if b < outer - 1 else last)
        core = core_ref[:, lanes] + dot(jnp.concatenate(scaled, axis=1), jnp.concatenate(stack, axis=0))
        core = core * lax.rsqrt(jnp.mean(core * core, axis=1, keepdims=True) + EPSILON)
        gate = gate_ref[:, lanes].astype(F32)
        normed.append((core * (gate / (1.0 + jnp.exp(-gate)))).astype(BF16))
    norm_ref[...] = jnp.concatenate(normed, axis=1)
    chunk = tokens // ring
    for j in range(ring):
        owner = lax.rem(pos_ref[1] + ring + ring // 2 - j, ring)
        turn_ref[j * chunk : (j + 1) * chunk] = norm_ref[pl.ds(pl.multiple_of(owner * chunk, chunk), chunk)]
    normed = turn_ref[...]
    step = 512
    for c in range(0, out_ref.shape[1], step):
        out_ref[:, c : c + step] = dot(normed, out_w_ref[:, c : c + step]).astype(BF16)


def call(body, out_shape, specs, flops, bytes_accessed, scratch=()):
    return pl.pallas_call(
        body,
        out_shape=out_shape,
        in_specs=specs,
        out_specs=jax.tree.map(lambda _: VMEM, out_shape),
        scratch_shapes=scratch,
        compiler_params=pltpu.CompilerParams(vmem_limit_bytes=VMEM_BYTES),
        cost_estimate=pl.CostEstimate(flops=flops, bytes_accessed=bytes_accessed, transcendentals=0),
    )


def ring_sum(partial, ring):
    chunk = partial.shape[0] // ring
    half = ring // 2
    right = [(i, (i + 1) % ring) for i in range(ring)]
    left = [(i, (i - 1) % ring) for i in range(ring)]

    def term(j):
        return lax.slice_in_dim(partial, j * chunk, (j + 1) * chunk).astype(F32)

    ahead = term(0).astype(BF16)
    behind = term(ring - 1).astype(BF16)
    for t in range(1, half):
        ahead = (lax.ppermute(ahead, "head", right).astype(F32) + term(t)).astype(BF16)
        if t < half - 1:
            behind = (lax.ppermute(behind, "head", left).astype(F32) + term(ring - 1 - t)).astype(BF16)
    ahead = lax.ppermute(ahead, "head", right).astype(F32)
    behind = lax.ppermute(behind, "head", left).astype(F32)
    return (ahead + behind + term(half)).astype(BF16)


def on_device(queries, keys, values, gate, log_forget, write_rate, level_weight, w_out):
    tokens = queries.shape[0]
    heads = log_forget.shape[0]
    seq = lax.axis_size("seq")
    outer = seq.bit_length() - 1
    ring = lax.axis_size("head")
    position = jnp.stack([lax.axis_index("seq"), lax.axis_index("head")]).astype(jnp.int32)
    wide = heads * DK

    def shape(dims, dtype=BF16):
        return jax.ShapeDtypeStruct(dims, dtype)

    total, inner, bases, writes, rows = call(
        states_kernel,
        (
            shape((heads, DK, 2 * DK)),
            shape((heads, 4, DK, 2 * DK)),
            shape((tokens, wide), F32),
            shape((tokens, wide), F32),
            shape((8, tokens), F32),
        ),
        [VMEM] * 4,
        2_000_000_000,
        1_000_000,
    )(keys, values, log_forget, write_rate)

    core, lifted = call(
        reads_kernel,
        (shape((tokens, wide), F32), shape((tokens, wide))),
        [VMEM] * 7,
        1_000_000_000,
        1_000_000,
    )(queries, keys, bases, writes, rows, inner, level_weight)

    before = jnp.zeros((heads, DK, DK), BF16) + jnp.eye(DK, dtype=BF16)
    collected = []
    for b in range(outer - 1):
        theirs = lax.ppermute(total, "seq", [(i, i ^ (1 << b)) for i in range(seq)])
        total, level, before = call(
            lambda *refs, b=b: merge_kernel(b, *refs),
            (shape((heads, DK, 2 * DK)), shape((heads, DK, DK)), shape((heads, DK, DK))),
            [SMEM] + [VMEM] * 3,
            40_000_000,
            500_000,
        )(position, total, theirs, before)
        collected.append(level)
    top = 1 << (outer - 1)
    last = lax.ppermute(total[:, :, :DK], "seq", [(i, i + top) for i in range(top)])
    partial = call(
        lambda *refs: final_kernel(outer, ring, *refs),
        shape((tokens, w_out.shape[1])),
        [SMEM] + [VMEM] * (7 + outer - 1),
        600_000_000,
        5_000_000,
        [pltpu.VMEM((tokens, wide), BF16)] * 2,
    )(position, core, lifted, last, before, level_weight, gate, w_out, *collected)
    return ring_sum(partial, ring)


def solution(mesh):
    in_specs = (
        P("seq", "head"),
        P("seq", "head"),
        P("seq", "head"),
        P("seq", "head"),
        P("head", "seq"),
        P("head", "seq"),
        P("head", None, "seq"),
        P("head", None),
    )
    out_specs = P(("seq", "head"), None)
    return jax.shard_map(
        on_device, mesh=mesh, in_specs=in_specs, out_specs=out_specs, check_vma=False
    )
```

```python
import jax
import jax.numpy as jnp
from jax import lax
from jax.experimental import pallas as pl
from jax.experimental.pallas import tpu as pltpu
from jax.sharding import PartitionSpec as P

DK = 128
BLOCK = 64
EPSILON = 1e-06
F32 = jnp.float32
BF16 = jnp.bfloat16
VMEM = pl.BlockSpec(memory_space=pltpu.VMEM)
SMEM = pl.BlockSpec(memory_space=pltpu.SMEM)
VMEM_BYTES = 48 * 1024 * 1024


def dot(left, right, dims=((1,), (0,)), precision=None):
    return lax.dot_general(left, right, (dims, ((), ())), precision=precision, preferred_element_type=F32)


def halves(matrix):
    high = matrix.astype(BF16)
    return high, (matrix - high.astype(F32)).astype(BF16)


def dot3(left, right):
    (lh, ll), (rh, rl) = left, right
    return dot(lh, rh) + (dot(lh, rl) + dot(ll, rh))


def dot2(left, right):
    high, low = halves(left)
    return dot(high, right) + dot(low, right)


def block_masks(tokens):
    row = lax.broadcasted_iota(jnp.int32, (tokens, tokens), 0)
    col = lax.broadcasted_iota(jnp.int32, (tokens, tokens), 1)
    same = row // BLOCK == col // BLOCK
    return row, col, same


def states_kernel(k_ref, v_ref, lf_ref, wr_ref, x_ref, y_ref, w_ref, u_ref, rows_ref):
    tokens = k_ref.shape[0]
    heads = lf_ref.shape[0]
    blocks = tokens // BLOCK
    row, col, same = block_masks(tokens)
    inclusive = same & (row >= col)
    strict = same & (row > col)
    eye = (row == col).astype(F32)
    log_forget = lf_ref[...]
    rate = wr_ref[...]
    exact = lax.Precision.HIGHEST
    cum = dot(log_forget, inclusive.astype(F32), ((1,), (1,)), exact)
    total = dot(log_forget, same.astype(F32), ((1,), (1,)), exact)
    pad = jnp.zeros((8 - 3 * heads, tokens), F32)
    columns = jnp.concatenate([cum, total, rate, pad], axis=0).T
    eye_state = (
        lax.broadcasted_iota(jnp.int32, (DK, DK), 0) == lax.broadcasted_iota(jnp.int32, (DK, DK), 1)
    ).astype(F32)
    inv_key_rows = []
    lowers, keys, norms = [], [], []
    for h in range(heads):
        key = k_ref[:, h * DK : (h + 1) * DK]
        key_f = key.astype(F32)
        key_key = dot(key, key, ((1,), (1,)))
        inv_col = lax.rsqrt(jnp.sum(key_f * key_f, axis=1, keepdims=True) + EPSILON)
        inv_row = lax.rsqrt(jnp.sum(key_key * eye, axis=0, keepdims=True) + EPSILON)
        inv_key_rows.append(inv_row)
        rate_col = columns[:, 2 * heads + h : 2 * heads + h + 1]
        lowers.append(jnp.where(strict, key_key * (rate_col * inv_col) * inv_row, 0.0))
        keys.append((key, key_f))
        norms.append((inv_col, inv_row))
    inverses = [eye - jnp.where(row // 2 == col // 2, lower, 0.0) for lower in lowers]
    width = 2
    while width < BLOCK:
        band = (row // width != col // width) & (row // (2 * width) == col // (2 * width))
        nexts = []
        for h in range(heads):
            inverse = halves(inverses[h])
            inner = dot3(halves(jnp.where(band, lowers[h], 0.0)), inverse)
            nexts.append(inverses[h] - dot3(inverse, halves(inner)))
        inverses = nexts
        width *= 2
    for h in range(heads):
        key, key_f = keys[h]
        inv_col, inv_row = norms[h]
        value = v_ref[:, h * DK : (h + 1) * DK]
        cum_row = cum[h : h + 1]
        cum_col = columns[:, h : h + 1]
        total_col = columns[:, heads + h : heads + h + 1]
        rate_row = rate[h : h + 1]
        fading = jnp.exp(jnp.where(inclusive, cum_col - cum_row, -1e30))
        solved = inverses[h] * rate_row
        bases = dot2(solved * inv_row, key)
        writes = dot2(solved * fading, value)
        w_ref[:, h * DK : (h + 1) * DK] = bases
        u_ref[:, h * DK : (h + 1) * DK] = writes
        both = jnp.concatenate(
            [writes * (jnp.exp(total_col - cum_col) * inv_col), bases * inv_col], axis=1
        )
        both_high, both_low = halves(both)
        leaf = []
        for g in range(blocks):
            span = slice(g * BLOCK, (g + 1) * BLOCK)
            turned = key_f[span].T.astype(BF16)
            raw = dot(turned, both_high[span]) + dot(turned, both_low[span])
            fade = jnp.exp(total[h : h + 1, g * BLOCK : g * BLOCK + 1])
            leaf.append(jnp.concatenate([raw[:, :DK], fade * (eye_state - raw[:, DK:])], axis=1))
        short = [x.astype(BF16) for x in leaf]

        def merge(lead, trail):
            moved = dot(trail[:, DK:].astype(BF16), lead.astype(BF16))
            return jnp.concatenate([moved[:, :DK] + trail[:, :DK], moved[:, DK:]], axis=1)

        first = merge(leaf[0], leaf[1])
        second = merge(leaf[2], leaf[3])
        y_ref[h, 0] = short[0]
        y_ref[h, 1] = first.astype(BF16)
        y_ref[h, 2] = dot(short[2][:, DK:], first.astype(BF16)).astype(BF16)
        y_ref[h, 3] = short[2]
        x_ref[h] = merge(first, second).astype(BF16)
    rows_ref[...] = jnp.concatenate([cum] + inv_key_rows + [jnp.zeros((8 - 2 * heads, tokens), F32)], axis=0)


def reads_kernel(q_ref, k_ref, w_ref, u_ref, rows_ref, y_ref, lw_ref, core_ref, lift_ref):
    tokens = k_ref.shape[0]
    heads = y_ref.shape[0]
    row, col, same = block_masks(tokens)
    inclusive = same & (row >= col)
    rows = rows_ref[...]
    columns = rows.T
    levels = lw_ref.shape[1]
    weights = lw_ref[...].reshape(heads * levels, tokens).T
    for h in range(heads):
        lanes = slice(h * DK, (h + 1) * DK)
        query = q_ref[:, lanes]
        key = k_ref[:, lanes]
        query_f = query.astype(F32)
        inv_query = lax.rsqrt(jnp.sum(query_f * query_f, axis=1, keepdims=True) + EPSILON)
        query_key = dot(query, key, ((1,), (1,))) * inv_query * rows[heads + h : heads + h + 1]
        cum_col = columns[:, h : h + 1]
        fading = jnp.exp(jnp.where(inclusive, cum_col - rows[h : h + 1], -1e30))
        own = dot3(halves(query_key * fading), halves(u_ref[:, lanes]))
        masked = jnp.where(inclusive, query_key, 0.0)
        reach = jnp.exp(cum_col) * (query_f * inv_query - dot3(halves(masked), halves(w_ref[:, lanes])))
        reach_s = reach.astype(BF16)

        def weight(level, span):
            at = h * levels + level
            return weights[span, at : at + 1]

        spans = [slice(g * BLOCK, (g + 1) * BLOCK) for g in range(4)]
        read1 = dot(reach_s[spans[1]], y_ref[h, 0])
        read2 = dot(reach_s[spans[2]], y_ref[h, 1])
        read3 = dot(reach_s[spans[3]], y_ref[h, 2])
        near3 = dot(reach_s[spans[3]], y_ref[h, 3, :, :DK])
        core_ref[spans[0], lanes] = weight(0, spans[0]) * own[spans[0]]
        core_ref[spans[1], lanes] = weight(0, spans[1]) * own[spans[1]] + weight(1, spans[1]) * read1[:, :DK]
        core_ref[spans[2], lanes] = weight(0, spans[2]) * own[spans[2]] + weight(2, spans[2]) * read2[:, :DK]
        core_ref[spans[3], lanes] = (
            weight(0, spans[3]) * own[spans[3]]
            + weight(1, spans[3]) * near3
            + weight(2, spans[3]) * read3[:, :DK]
        )
        lift_ref[spans[0], lanes] = reach_s[spans[0]]
        lift_ref[spans[1], lanes] = read1[:, DK:].astype(BF16)
        lift_ref[spans[2], lanes] = read2[:, DK:].astype(BF16)
        lift_ref[spans[3], lanes] = read3[:, DK:].astype(BF16)


def merge_kernel(bit, pos_ref, mine_ref, theirs_ref, before_ref, total_ref, level_ref, after_ref):
    upper = (pos_ref[0] >> bit) & 1 == 1
    heads = mine_ref.shape[0]

    def joined(lead, trail):
        moved = dot(trail[:, DK:], lead)
        return jnp.concatenate([moved[:, :DK] + trail[:, :DK].astype(F32), moved[:, DK:]], axis=1).astype(BF16)

    @pl.when(upper)
    def _():
        for h in range(heads):
            total_ref[h] = joined(theirs_ref[h], mine_ref[h])
        for h in range(heads):
            if bit == 0:
                level_ref[h] = theirs_ref[h, :, :DK]
                after_ref[h] = theirs_ref[h, :, DK:]
            else:
                read = dot(before_ref[h], theirs_ref[h]).astype(BF16)
                level_ref[h] = read[:, :DK]
                after_ref[h] = read[:, DK:]

    @pl.when(jnp.logical_not(upper))
    def _():
        for h in range(heads):
            total_ref[h] = joined(mine_ref[h], theirs_ref[h])
        level_ref[...] = jnp.zeros(level_ref.shape, level_ref.dtype)
        after_ref[...] = before_ref[...]


def finish_kernel(outer, ring, pos_ref, core_ref, lift_ref, last_ref, before_ref, lw_ref, gate_ref, *rest):
    level_refs, keep_ref, give_ref, norm_ref = rest[:-3], rest[-3], rest[-2], rest[-1]
    heads = before_ref.shape[0]
    tokens = core_ref.shape[0]
    levels = lw_ref.shape[1]
    weights = lw_ref[...].reshape(heads * levels, tokens).T
    upper = ((pos_ref[0] >> (outer - 1)) & 1 == 1).astype(F32)
    for h in range(heads):
        lanes = slice(h * DK, (h + 1) * DK)
        lifted = lift_ref[:, lanes].astype(F32)
        last = (dot(before_ref[h], last_ref[h]) * upper).astype(BF16)
        scaled, stack = [], []
        for b in range(outer):
            at = h * levels + levels - outer + b
            scaled.append((lifted * weights[:, at : at + 1]).astype(BF16))
            stack.append(level_refs[b][h] if b < outer - 1 else last)
        core = core_ref[:, lanes] + dot(jnp.concatenate(scaled, axis=1), jnp.concatenate(stack, axis=0))
        core = core * lax.rsqrt(jnp.mean(core * core, axis=1, keepdims=True) + EPSILON)
        gate = gate_ref[:, lanes].astype(F32)
        norm_ref[:, lanes] = (core * (gate / (1.0 + jnp.exp(-gate)))).astype(BF16)
    chunk = tokens // (2 * ring)
    pair = pos_ref[1] // 2
    parity = lax.rem(pos_ref[1], 2)
    for j in range(ring):
        owner = 2 * lax.rem(pair + ring + ring // 2 - j, ring)
        rows = slice(j * chunk, (j + 1) * chunk)
        keep_ref[rows] = norm_ref[pl.ds(pl.multiple_of((owner + parity) * chunk, chunk), chunk)]
        give_ref[rows] = norm_ref[pl.ds(pl.multiple_of((owner + 1 - parity) * chunk, chunk), chunk)]


def project_kernel(keep_ref, got_ref, mine_ref, theirs_ref, *out_refs):
    sums = dot(keep_ref[...], mine_ref[...]) + dot(got_ref[...], theirs_ref[...])
    chunk = out_refs[0].shape[0]
    for j, out_ref in enumerate(out_refs):
        out_ref[...] = sums[j * chunk : (j + 1) * chunk].astype(BF16)


def call(body, out_shape, specs, flops, bytes_accessed, scratch=()):
    return pl.pallas_call(
        body,
        out_shape=out_shape,
        in_specs=specs,
        out_specs=jax.tree.map(lambda _: VMEM, out_shape),
        scratch_shapes=scratch,
        compiler_params=pltpu.CompilerParams(vmem_limit_bytes=VMEM_BYTES),
        cost_estimate=pl.CostEstimate(flops=flops, bytes_accessed=bytes_accessed, transcendentals=0),
    )


def ring_sum(terms):
    ring = len(terms)
    half = ring // 2
    count = 2 * ring
    right = [(i, (i + 2) % count) for i in range(count)]
    left = [(i, (i - 2) % count) for i in range(count)]
    ahead, behind = terms[0], terms[ring - 1]
    for t in range(1, half):
        ahead = (lax.ppermute(ahead, "head", right).astype(F32) + terms[t].astype(F32)).astype(BF16)
        if t < half - 1:
            behind = (lax.ppermute(behind, "head", left).astype(F32) + terms[ring - 1 - t].astype(F32)).astype(BF16)
    ahead = lax.ppermute(ahead, "head", right).astype(F32)
    behind = lax.ppermute(behind, "head", left).astype(F32)
    return (ahead + behind + terms[half].astype(F32)).astype(BF16)


def on_device(queries, keys, values, gate, log_forget, write_rate, level_weight, w_out):
    tokens = queries.shape[0]
    heads = log_forget.shape[0]
    seq = lax.axis_size("seq")
    outer = seq.bit_length() - 1
    ring = lax.axis_size("head")
    position = jnp.stack([lax.axis_index("seq"), lax.axis_index("head")]).astype(jnp.int32)
    wide = heads * DK
    pairs = [(i, i ^ 1) for i in range(ring)]
    w_pair = lax.ppermute(w_out, "head", pairs)

    def shape(dims, dtype=BF16):
        return jax.ShapeDtypeStruct(dims, dtype)

    total, inner, bases, writes, rows = call(
        states_kernel,
        (
            shape((heads, DK, 2 * DK)),
            shape((heads, 4, DK, 2 * DK)),
            shape((tokens, wide), F32),
            shape((tokens, wide), F32),
            shape((8, tokens), F32),
        ),
        [VMEM] * 4,
        2_000_000_000,
        1_000_000,
    )(keys, values, log_forget, write_rate)

    core, lifted = call(
        reads_kernel,
        (shape((tokens, wide), F32), shape((tokens, wide))),
        [VMEM] * 7,
        1_000_000_000,
        1_000_000,
    )(queries, keys, bases, writes, rows, inner, level_weight)

    before = jnp.zeros((heads, DK, DK), BF16) + jnp.eye(DK, dtype=BF16)
    collected = []
    for b in range(outer - 1):
        theirs = lax.ppermute(total, "seq", [(i, i ^ (1 << b)) for i in range(seq)])
        total, level, before = call(
            lambda *refs, b=b: merge_kernel(b, *refs),
            (shape((heads, DK, 2 * DK)), shape((heads, DK, DK)), shape((heads, DK, DK))),
            [SMEM] + [VMEM] * 3,
            40_000_000,
            500_000,
        )(position, total, theirs, before)
        collected.append(level)
    top = 1 << (outer - 1)
    last = lax.ppermute(total[:, :, :DK], "seq", [(i, i + top) for i in range(top)])
    keep, give = call(
        lambda *refs: finish_kernel(outer, ring // 2, *refs),
        (shape((tokens // 2, wide)), shape((tokens // 2, wide))),
        [SMEM] + [VMEM] * (6 + outer - 1),
        100_000_000,
        1_000_000,
        [pltpu.VMEM((tokens, wide), BF16)],
    )(position, core, lifted, last, before, level_weight, gate, *collected)
    got = lax.ppermute(give, "head", pairs)
    columns = w_out.shape[1]
    step = columns // 4
    chunk = tokens // ring
    whole = pl.BlockSpec((tokens // 2, wide), lambda c: (0, 0))
    block = pl.BlockSpec((wide, step), lambda c: (0, c))
    terms = pl.pallas_call(
        project_kernel,
        grid=(columns // step,),
        out_shape=[shape((chunk, columns))] * (ring // 2),
        in_specs=[whole, whole, block, block],
        out_specs=[pl.BlockSpec((chunk, step), lambda c: (0, c))] * (ring // 2),
        compiler_params=pltpu.CompilerParams(vmem_limit_bytes=VMEM_BYTES),
        cost_estimate=pl.CostEstimate(flops=600_000_000, bytes_accessed=6_000_000, transcendentals=0),
    )(keep, got, w_out, w_pair)
    return ring_sum(terms)


def solution(mesh):
    in_specs = (
        P("seq", "head"),
        P("seq", "head"),
        P("seq", "head"),
        P("seq", "head"),
        P("head", "seq"),
        P("head", "seq"),
        P("head", None, "seq"),
        P("head", None),
    )
    out_specs = P(("seq", "head"), None)
    return jax.shard_map(
        on_device, mesh=mesh, in_specs=in_specs, out_specs=out_specs, check_vma=False
    )
```

```python
import jax
import jax.numpy as jnp
from jax import lax
from jax.experimental import pallas as pl
from jax.experimental.pallas import tpu as pltpu
from jax.sharding import PartitionSpec as P

DK = 128
BLOCK = 64
EPSILON = 1e-06
F32 = jnp.float32
BF16 = jnp.bfloat16
VMEM = pl.BlockSpec(memory_space=pltpu.VMEM)
SMEM = pl.BlockSpec(memory_space=pltpu.SMEM)
VMEM_BYTES = 48 * 1024 * 1024


def dot(left, right, dims=((1,), (0,)), precision=None):
    return lax.dot_general(left, right, (dims, ((), ())), precision=precision, preferred_element_type=F32)


def halves(matrix):
    high = matrix.astype(BF16)
    return high, (matrix - high.astype(F32)).astype(BF16)


def dot3(left, right):
    (lh, ll), (rh, rl) = left, right
    return dot(lh, rh) + (dot(lh, rl) + dot(ll, rh))


def dot2(left, right):
    high, low = halves(left)
    return dot(high, right) + dot(low, right)


def block_masks(tokens):
    row = lax.broadcasted_iota(jnp.int32, (tokens, tokens), 0)
    col = lax.broadcasted_iota(jnp.int32, (tokens, tokens), 1)
    same = row // BLOCK == col // BLOCK
    return row, col, same


def states_kernel(k_ref, v_ref, lf_ref, wr_ref, x_ref, y_ref, w_ref, u_ref, rows_ref):
    tokens = k_ref.shape[0]
    heads = lf_ref.shape[0]
    blocks = tokens // BLOCK
    row, col, same = block_masks(tokens)
    inclusive = same & (row >= col)
    strict = same & (row > col)
    eye = (row == col).astype(F32)
    log_forget = lf_ref[...]
    rate = wr_ref[...]
    exact = lax.Precision.HIGHEST
    cum = dot(log_forget, inclusive.astype(F32), ((1,), (1,)), exact)
    total = dot(log_forget, same.astype(F32), ((1,), (1,)), exact)
    pad = jnp.zeros((8 - 3 * heads, tokens), F32)
    columns = jnp.concatenate([cum, total, rate, pad], axis=0).T
    eye_state = (
        lax.broadcasted_iota(jnp.int32, (DK, DK), 0) == lax.broadcasted_iota(jnp.int32, (DK, DK), 1)
    ).astype(F32)
    inv_key_rows = []
    lowers, keys, norms = [], [], []
    for h in range(heads):
        key = k_ref[:, h * DK : (h + 1) * DK]
        key_f = key.astype(F32)
        key_key = dot(key, key, ((1,), (1,)))
        inv_col = lax.rsqrt(jnp.sum(key_f * key_f, axis=1, keepdims=True) + EPSILON)
        inv_row = lax.rsqrt(jnp.sum(key_key * eye, axis=0, keepdims=True) + EPSILON)
        inv_key_rows.append(inv_row)
        rate_col = columns[:, 2 * heads + h : 2 * heads + h + 1]
        lowers.append(jnp.where(strict, key_key * (rate_col * inv_col) * inv_row, 0.0))
        keys.append((key, key_f))
        norms.append((inv_col, inv_row))
    inverses = [eye - jnp.where(row // 2 == col // 2, lower, 0.0) for lower in lowers]
    width = 2
    while width < BLOCK:
        band = (row // width != col // width) & (row // (2 * width) == col // (2 * width))
        nexts = []
        for h in range(heads):
            inverse = halves(inverses[h])
            inner = dot3(halves(jnp.where(band, lowers[h], 0.0)), inverse)
            nexts.append(inverses[h] - dot3(inverse, halves(inner)))
        inverses = nexts
        width *= 2
    for h in range(heads):
        key, key_f = keys[h]
        inv_col, inv_row = norms[h]
        value = v_ref[:, h * DK : (h + 1) * DK]
        cum_row = cum[h : h + 1]
        cum_col = columns[:, h : h + 1]
        total_col = columns[:, heads + h : heads + h + 1]
        rate_row = rate[h : h + 1]
        fading = jnp.exp(jnp.where(inclusive, cum_col - cum_row, -1e30))
        solved = inverses[h] * rate_row
        bases = dot2(solved * inv_row, key)
        writes = dot2(solved * fading, value)
        w_ref[:, h * DK : (h + 1) * DK] = bases
        u_ref[:, h * DK : (h + 1) * DK] = writes
        both = jnp.concatenate(
            [writes * (jnp.exp(total_col - cum_col) * inv_col), bases * inv_col], axis=1
        )
        both_high, both_low = halves(both)
        leaf = []
        for g in range(blocks):
            span = slice(g * BLOCK, (g + 1) * BLOCK)
            turned = key_f[span].T.astype(BF16)
            raw = dot(turned, both_high[span]) + dot(turned, both_low[span])
            fade = jnp.exp(total[h : h + 1, g * BLOCK : g * BLOCK + 1])
            leaf.append(jnp.concatenate([raw[:, :DK], fade * (eye_state - raw[:, DK:])], axis=1))
        short = [x.astype(BF16) for x in leaf]

        def merge(lead, trail):
            moved = dot(trail[:, DK:].astype(BF16), lead.astype(BF16))
            return jnp.concatenate([moved[:, :DK] + trail[:, :DK], moved[:, DK:]], axis=1)

        first = merge(leaf[0], leaf[1])
        second = merge(leaf[2], leaf[3])
        y_ref[h, 0] = short[0]
        y_ref[h, 1] = first.astype(BF16)
        y_ref[h, 2] = dot(short[2][:, DK:], first.astype(BF16)).astype(BF16)
        y_ref[h, 3] = short[2]
        x_ref[h] = merge(first, second).astype(BF16)
    rows_ref[...] = jnp.concatenate([cum] + inv_key_rows + [jnp.zeros((8 - 2 * heads, tokens), F32)], axis=0)


def reads_kernel(q_ref, k_ref, w_ref, u_ref, rows_ref, y_ref, lw_ref, core_ref, lift_ref):
    tokens = k_ref.shape[0]
    heads = y_ref.shape[0]
    row, col, same = block_masks(tokens)
    inclusive = same & (row >= col)
    rows = rows_ref[...]
    columns = rows.T
    levels = lw_ref.shape[1]
    weights = lw_ref[...].reshape(heads * levels, tokens).T
    for h in range(heads):
        lanes = slice(h * DK, (h + 1) * DK)
        query = q_ref[:, lanes]
        key = k_ref[:, lanes]
        query_f = query.astype(F32)
        inv_query = lax.rsqrt(jnp.sum(query_f * query_f, axis=1, keepdims=True) + EPSILON)
        query_key = dot(query, key, ((1,), (1,))) * inv_query * rows[heads + h : heads + h + 1]
        cum_col = columns[:, h : h + 1]
        fading = jnp.exp(jnp.where(inclusive, cum_col - rows[h : h + 1], -1e30))
        own = dot3(halves(query_key * fading), halves(u_ref[:, lanes]))
        masked = jnp.where(inclusive, query_key, 0.0)
        reach = jnp.exp(cum_col) * (query_f * inv_query - dot3(halves(masked), halves(w_ref[:, lanes])))
        reach_s = reach.astype(BF16)

        def weight(level, span):
            at = h * levels + level
            return weights[span, at : at + 1]

        spans = [slice(g * BLOCK, (g + 1) * BLOCK) for g in range(4)]
        read1 = dot(reach_s[spans[1]], y_ref[h, 0])
        read2 = dot(reach_s[spans[2]], y_ref[h, 1])
        read3 = dot(reach_s[spans[3]], y_ref[h, 2])
        near3 = dot(reach_s[spans[3]], y_ref[h, 3, :, :DK])
        core_ref[spans[0], lanes] = weight(0, spans[0]) * own[spans[0]]
        core_ref[spans[1], lanes] = weight(0, spans[1]) * own[spans[1]] + weight(1, spans[1]) * read1[:, :DK]
        core_ref[spans[2], lanes] = weight(0, spans[2]) * own[spans[2]] + weight(2, spans[2]) * read2[:, :DK]
        core_ref[spans[3], lanes] = (
            weight(0, spans[3]) * own[spans[3]]
            + weight(1, spans[3]) * near3
            + weight(2, spans[3]) * read3[:, :DK]
        )
        lift_ref[spans[0], lanes] = reach_s[spans[0]]
        lift_ref[spans[1], lanes] = read1[:, DK:].astype(BF16)
        lift_ref[spans[2], lanes] = read2[:, DK:].astype(BF16)
        lift_ref[spans[3], lanes] = read3[:, DK:].astype(BF16)


def merge_kernel(pos_ref, mine_ref, theirs_ref, total_ref, level_ref, after_ref):
    upper = lax.rem(pos_ref[0], 2) == 1
    same = lax.broadcasted_iota(jnp.int32, (DK, DK), 0) == lax.broadcasted_iota(jnp.int32, (DK, DK), 1)
    for h in range(mine_ref.shape[0]):
        mine, theirs = mine_ref[h], theirs_ref[h]
        total_ref[h] = joined(jnp.where(upper, theirs, mine), jnp.where(upper, mine, theirs))
        level_ref[h] = jnp.where(upper, theirs[:, :DK], jnp.zeros((DK, DK), BF16))
        after_ref[h] = jnp.where(upper, theirs[:, DK:], same.astype(BF16))


def joined(lead, trail):
    moved = dot(trail[:, DK:], lead)
    return jnp.concatenate([moved[:, :DK] + trail[:, :DK].astype(F32), moved[:, DK:]], axis=1).astype(BF16)


def two_levels(digit, four_ref, before_ref, h):
    before = before_ref[h]
    near = dot(before, four_ref[jnp.maximum(digit - 1, 0), h]).astype(BF16)
    odd = lax.rem(digit, 2) == 1
    low = jnp.where(odd, near[:, :DK], jnp.zeros((DK, DK), BF16))
    before = jnp.where(odd, near[:, DK:], before)
    first = joined(four_ref[0, h], four_ref[1, h])
    far = dot(before, first).astype(BF16)
    upper = digit >= 2
    high = jnp.where(upper, far[:, :DK], jnp.zeros((DK, DK), BF16))
    return low, high, jnp.where(upper, far[:, DK:], before), first


def quad_kernel(bit, pos_ref, four_ref, before_ref, total_ref, low_ref, high_ref, after_ref):
    digit = (pos_ref[0] >> bit) & 3
    for h in range(before_ref.shape[0]):
        low_ref[h], high_ref[h], after_ref[h], first = two_levels(digit, four_ref, before_ref, h)
        total_ref[h] = joined(first, joined(four_ref[2, h], four_ref[3, h]))


def finish_kernel(outer, ring, pos_ref, core_ref, lift_ref, four_ref, before_ref, lw_ref, gate_ref, *rest):
    level_refs, keep_ref, give_ref, norm_ref = rest[:-3], rest[-3], rest[-2], rest[-1]
    digit = (pos_ref[0] >> (outer - 2)) & 3
    heads = before_ref.shape[0]
    tokens = core_ref.shape[0]
    levels = lw_ref.shape[1]
    weights = lw_ref[...].reshape(heads * levels, tokens).T
    for h in range(heads):
        lanes = slice(h * DK, (h + 1) * DK)
        lifted = lift_ref[:, lanes].astype(F32)
        low, high, _, _ = two_levels(digit, four_ref, before_ref, h)
        stack = [level_ref[h] for level_ref in level_refs] + [low, high]
        scaled = []
        for b in range(outer):
            at = h * levels + levels - outer + b
            scaled.append((lifted * weights[:, at : at + 1]).astype(BF16))
        core = core_ref[:, lanes] + dot(jnp.concatenate(scaled, axis=1), jnp.concatenate(stack, axis=0))
        core = core * lax.rsqrt(jnp.mean(core * core, axis=1, keepdims=True) + EPSILON)
        gate = gate_ref[:, lanes].astype(F32)
        norm_ref[:, lanes] = (core * (gate / (1.0 + jnp.exp(-gate)))).astype(BF16)
    side = 1 - 2 * lax.rem(pos_ref[0], 2)
    chunk = tokens // (2 * ring)
    pair = pos_ref[1] // 2
    parity = lax.rem(pos_ref[1], 2)
    for j in range(ring):
        owner = 2 * lax.rem(pair + ring + side * (ring // 2 - j), ring)
        rows = slice(j * chunk, (j + 1) * chunk)
        keep_ref[rows] = norm_ref[pl.ds(pl.multiple_of((owner + parity) * chunk, chunk), chunk)]
        give_ref[rows] = norm_ref[pl.ds(pl.multiple_of((owner + 1 - parity) * chunk, chunk), chunk)]


def project_kernel(keep_ref, got_ref, mine_ref, theirs_ref, *out_refs):
    sums = dot(keep_ref[...], mine_ref[...]) + dot(got_ref[...], theirs_ref[...])
    chunk = out_refs[0].shape[0]
    for j, out_ref in enumerate(out_refs):
        out_ref[...] = sums[j * chunk : (j + 1) * chunk].astype(BF16)


def call(body, out_shape, specs, flops, bytes_accessed, scratch=()):
    return pl.pallas_call(
        body,
        out_shape=out_shape,
        in_specs=specs,
        out_specs=jax.tree.map(lambda _: VMEM, out_shape),
        scratch_shapes=scratch,
        compiler_params=pltpu.CompilerParams(vmem_limit_bytes=VMEM_BYTES),
        cost_estimate=pl.CostEstimate(flops=flops, bytes_accessed=bytes_accessed, transcendentals=0),
    )


def ring_sum(terms):
    ring = len(terms)
    half = ring // 2
    count = 2 * ring
    slabs = lax.axis_size("seq")

    def hop(block, way):
        route = []
        for s in range(slabs):
            step = 2 * way * (1 - 2 * (s % 2))
            route += [(s * count + z, s * count + (z + step) % count) for z in range(count)]
        return lax.ppermute(block, ("seq", "head"), route).astype(F32)

    ahead, behind = terms[0], terms[ring - 1]
    for t in range(1, half):
        ahead = (hop(ahead, 1) + terms[t].astype(F32)).astype(BF16)
        if t < half - 1:
            behind = (hop(behind, -1) + terms[ring - 1 - t].astype(F32)).astype(BF16)
    ahead = hop(ahead, 1) + terms[half].astype(F32)
    return (ahead + hop(behind, -1) if half > 1 else ahead).astype(BF16)


def on_device(queries, keys, values, gate, log_forget, write_rate, level_weight, w_out):
    tokens = queries.shape[0]
    heads = log_forget.shape[0]
    seq = lax.axis_size("seq")
    outer = seq.bit_length() - 1
    ring = lax.axis_size("head")
    position = jnp.stack([lax.axis_index("seq"), lax.axis_index("head")]).astype(jnp.int32)
    wide = heads * DK
    pairs = [(i, i ^ 1) for i in range(ring)]
    w_pair = lax.ppermute(w_out, "head", pairs)

    def shape(dims, dtype=BF16):
        return jax.ShapeDtypeStruct(dims, dtype)

    total, inner, bases, writes, rows = call(
        states_kernel,
        (
            shape((heads, DK, 2 * DK)),
            shape((heads, 4, DK, 2 * DK)),
            shape((tokens, wide), F32),
            shape((tokens, wide), F32),
            shape((8, tokens), F32),
        ),
        [VMEM] * 4,
        2_000_000_000,
        1_000_000,
    )(keys, values, log_forget, write_rate)

    core, lifted = call(
        reads_kernel,
        (shape((tokens, wide), F32), shape((tokens, wide))),
        [VMEM] * 7,
        1_000_000_000,
        1_000_000,
    )(queries, keys, bases, writes, rows, inner, level_weight)

    theirs = lax.ppermute(total, "seq", [(i, i ^ 1) for i in range(seq)])
    matrix = shape((heads, DK, DK))
    total, level, before = call(
        merge_kernel,
        (shape((heads, DK, 2 * DK)), matrix, matrix),
        [SMEM] + [VMEM] * 2,
        40_000_000,
        500_000,
    )(position, total, theirs)
    collected = [level]

    def gathered(b):
        stride = 1 << b
        groups = [[i + k * stride for k in range(4)] for i in range(seq) if (i >> b) & 3 == 0]
        return lax.all_gather(total, "seq", axis=0, axis_index_groups=groups)

    for b in range(1, outer - 2, 2):
        total, low, high, before = call(
            lambda *refs, b=b: quad_kernel(b, *refs),
            (shape((heads, DK, 2 * DK)), matrix, matrix, matrix),
            [SMEM] + [VMEM] * 2,
            100_000_000,
            1_000_000,
        )(position, gathered(b), before)
        collected += [low, high]
    four = gathered(outer - 2)
    keep, give = call(
        lambda *refs: finish_kernel(outer, ring // 2, *refs),
        (shape((tokens // 2, wide)), shape((tokens // 2, wide))),
        [SMEM] + [VMEM] * (6 + outer - 2),
        100_000_000,
        1_000_000,
        [pltpu.VMEM((tokens, wide), BF16)],
    )(position, core, lifted, four, before, level_weight, gate, *collected)
    got = lax.ppermute(give, "head", pairs)
    columns = w_out.shape[1]
    step = columns // 4
    chunk = tokens // ring
    whole = pl.BlockSpec((tokens // 2, wide), lambda c: (0, 0))
    block = pl.BlockSpec((wide, step), lambda c: (0, c))
    terms = pl.pallas_call(
        project_kernel,
        grid=(columns // step,),
        out_shape=[shape((chunk, columns))] * (ring // 2),
        in_specs=[whole, whole, block, block],
        out_specs=[pl.BlockSpec((chunk, step), lambda c: (0, c))] * (ring // 2),
        compiler_params=pltpu.CompilerParams(vmem_limit_bytes=VMEM_BYTES),
        cost_estimate=pl.CostEstimate(flops=600_000_000, bytes_accessed=6_000_000, transcendentals=0),
    )(keep, got, w_out, w_pair)
    return ring_sum(terms)


def solution(mesh):
    in_specs = (
        P("seq", "head"),
        P("seq", "head"),
        P("seq", "head"),
        P("seq", "head"),
        P("head", "seq"),
        P("head", "seq"),
        P("head", None, "seq"),
        P("head", None),
    )
    out_specs = P(("seq", "head"), None)
    return jax.shard_map(
        on_device, mesh=mesh, in_specs=in_specs, out_specs=out_specs, check_vma=False
    )
```

```python
import jax
import jax.numpy as jnp
from jax import lax
from jax.experimental import pallas as pl
from jax.experimental.pallas import tpu as pltpu
from jax.sharding import PartitionSpec as P

DK = 128
BLOCK = 64
EPSILON = 1e-06
F32 = jnp.float32
BF16 = jnp.bfloat16
VMEM = pl.BlockSpec(memory_space=pltpu.VMEM)
HBM = pl.BlockSpec(memory_space=pltpu.HBM)


def dot(left, right, dims=((1,), (0,)), precision=None):
    return lax.dot_general(left, right, (dims, ((), ())), precision=precision, preferred_element_type=F32)


def halves(matrix):
    high = matrix.astype(BF16)
    return high, (matrix - high.astype(F32)).astype(BF16)


def dot3(left, right):
    (lh, ll), (rh, rl) = left, right
    return dot(lh, rh) + (dot(lh, rl) + dot(ll, rh))


def dot2(left, right):
    high, low = halves(left)
    return dot(high, right) + dot(low, right)


def block_masks(tokens):
    row = lax.broadcasted_iota(jnp.int32, (tokens, tokens), 0)
    col = lax.broadcasted_iota(jnp.int32, (tokens, tokens), 1)
    same = row // BLOCK == col // BLOCK
    return row, col, same


def states_kernel(
    k_in, v_in, lf_in, wr_in, full_ref, x_ref, y_ref, w_ref, u_ref, rows_ref, half_ref,
    k_ref, v_ref, lf_ref, wr_ref, in_sems, half_sem,
):
    copies = [
        pltpu.make_async_copy(source, target, in_sems.at[i])
        for i, (source, target) in enumerate(((k_in, k_ref), (lf_in, lf_ref), (wr_in, wr_ref), (v_in, v_ref)))
    ]
    for copy in copies:
        copy.start()
    count = half_ref.shape[0]
    first = pl.multiple_of(lax.rem(lax.axis_index("seq"), 2) * count, count)
    half = pltpu.make_async_copy(full_ref.at[pl.ds(first, count)], half_ref, half_sem)
    half.start()
    for copy in copies:
        copy.wait()
    tokens = k_ref.shape[0]
    heads = lf_ref.shape[0]
    blocks = tokens // BLOCK
    row, col, same = block_masks(tokens)
    inclusive = same & (row >= col)
    strict = same & (row > col)
    eye = (row == col).astype(F32)
    log_forget = lf_ref[...]
    rate = wr_ref[...]
    exact = lax.Precision.HIGHEST
    cum = dot(log_forget, inclusive.astype(F32), ((1,), (1,)), exact)
    total = dot(log_forget, same.astype(F32), ((1,), (1,)), exact)
    pad = jnp.zeros((8 - 3 * heads, tokens), F32)
    columns = jnp.concatenate([cum, total, rate, pad], axis=0).T
    eye_state = (
        lax.broadcasted_iota(jnp.int32, (DK, DK), 0) == lax.broadcasted_iota(jnp.int32, (DK, DK), 1)
    ).astype(F32)
    inv_key_rows = []
    lowers, keys, norms = [], [], []
    for h in range(heads):
        key = k_ref[:, h * DK : (h + 1) * DK]
        key_f = key.astype(F32)
        key_key = dot(key, key, ((1,), (1,)))
        inv_col = lax.rsqrt(jnp.sum(key_f * key_f, axis=1, keepdims=True) + EPSILON)
        inv_row = lax.rsqrt(jnp.sum(key_key * eye, axis=0, keepdims=True) + EPSILON)
        inv_key_rows.append(inv_row)
        rate_col = columns[:, 2 * heads + h : 2 * heads + h + 1]
        lowers.append(jnp.where(strict, key_key * (rate_col * inv_col) * inv_row, 0.0))
        keys.append((key, key_f))
        norms.append((inv_col, inv_row))
    inverses = [eye - jnp.where(row // 2 == col // 2, lower, 0.0) for lower in lowers]
    width = 2
    while width < BLOCK:
        band = (row // width != col // width) & (row // (2 * width) == col // (2 * width))
        nexts = []
        for h in range(heads):
            inverse = halves(inverses[h])
            inner = dot3(halves(jnp.where(band, lowers[h], 0.0)), inverse)
            nexts.append(inverses[h] - dot3(inverse, halves(inner)))
        inverses = nexts
        width *= 2
    for h in range(heads):
        key, key_f = keys[h]
        inv_col, inv_row = norms[h]
        value = v_ref[:, h * DK : (h + 1) * DK]
        cum_row = cum[h : h + 1]
        cum_col = columns[:, h : h + 1]
        total_col = columns[:, heads + h : heads + h + 1]
        rate_row = rate[h : h + 1]
        fading = jnp.exp(jnp.where(inclusive, cum_col - cum_row, -1e30))
        solved = inverses[h] * rate_row
        bases = dot2(solved * inv_row, key)
        writes = dot2(solved * fading, value)
        w_ref[:, h * DK : (h + 1) * DK] = bases
        u_ref[:, h * DK : (h + 1) * DK] = writes
        both = jnp.concatenate(
            [writes * (jnp.exp(total_col - cum_col) * inv_col), bases * inv_col], axis=1
        )
        both_high, both_low = halves(both)
        leaf = []
        for g in range(blocks):
            span = slice(g * BLOCK, (g + 1) * BLOCK)
            turned = key_f[span].T.astype(BF16)
            raw = dot(turned, both_high[span]) + dot(turned, both_low[span])
            fade = jnp.exp(total[h : h + 1, g * BLOCK : g * BLOCK + 1])
            leaf.append(jnp.concatenate([raw[:, :DK], fade * (eye_state - raw[:, DK:])], axis=1))
        short = [x.astype(BF16) for x in leaf]

        def merge(lead, trail):
            moved = dot(trail[:, DK:].astype(BF16), lead.astype(BF16))
            return jnp.concatenate([moved[:, :DK] + trail[:, :DK], moved[:, DK:]], axis=1)

        first = merge(leaf[0], leaf[1])
        second = merge(leaf[2], leaf[3])
        y_ref[h, 0] = short[0]
        y_ref[h, 1] = first.astype(BF16)
        y_ref[h, 2] = dot(short[2][:, DK:], first.astype(BF16)).astype(BF16)
        y_ref[h, 3] = short[2]
        x_ref[h] = merge(first, second).astype(BF16)
    half.wait()
    rows_ref[...] = jnp.concatenate([cum] + inv_key_rows + [jnp.zeros((8 - 2 * heads, tokens), F32)], axis=0)


def reads_kernel(q_ref, k_ref, w_ref, u_ref, rows_ref, y_ref, lw_ref, core_ref, lift_ref):
    tokens = k_ref.shape[0]
    heads = y_ref.shape[0]
    row, col, same = block_masks(tokens)
    inclusive = same & (row >= col)
    rows = rows_ref[...]
    columns = rows.T
    levels = lw_ref.shape[1]
    weights = lw_ref[...].reshape(heads * levels, tokens).T
    for h in range(heads):
        lanes = slice(h * DK, (h + 1) * DK)
        query = q_ref[:, lanes]
        key = k_ref[:, lanes]
        query_f = query.astype(F32)
        inv_query = lax.rsqrt(jnp.sum(query_f * query_f, axis=1, keepdims=True) + EPSILON)
        query_key = dot(query, key, ((1,), (1,))) * inv_query * rows[heads + h : heads + h + 1]
        cum_col = columns[:, h : h + 1]
        fading = jnp.exp(jnp.where(inclusive, cum_col - rows[h : h + 1], -1e30))
        own = dot3(halves(query_key * fading), halves(u_ref[:, lanes]))
        masked = jnp.where(inclusive, query_key, 0.0)
        reach = jnp.exp(cum_col) * (query_f * inv_query - dot3(halves(masked), halves(w_ref[:, lanes])))
        reach_s = reach.astype(BF16)

        def weight(level, span):
            at = h * levels + level
            return weights[span, at : at + 1]

        spans = [slice(g * BLOCK, (g + 1) * BLOCK) for g in range(4)]
        read1 = dot(reach_s[spans[1]], y_ref[h, 0])
        read2 = dot(reach_s[spans[2]], y_ref[h, 1])
        read3 = dot(reach_s[spans[3]], y_ref[h, 2])
        near3 = dot(reach_s[spans[3]], y_ref[h, 3, :, :DK])
        core_ref[spans[0], lanes] = weight(0, spans[0]) * own[spans[0]]
        core_ref[spans[1], lanes] = weight(0, spans[1]) * own[spans[1]] + weight(1, spans[1]) * read1[:, :DK]
        core_ref[spans[2], lanes] = weight(0, spans[2]) * own[spans[2]] + weight(2, spans[2]) * read2[:, :DK]
        core_ref[spans[3], lanes] = (
            weight(0, spans[3]) * own[spans[3]]
            + weight(1, spans[3]) * near3
            + weight(2, spans[3]) * read3[:, :DK]
        )
        lift_ref[spans[0], lanes] = reach_s[spans[0]]
        lift_ref[spans[1], lanes] = read1[:, DK:].astype(BF16)
        lift_ref[spans[2], lanes] = read2[:, DK:].astype(BF16)
        lift_ref[spans[3], lanes] = read3[:, DK:].astype(BF16)


def merge_kernel(mine_ref, theirs_ref, total_ref, level_ref, after_ref):
    upper = lax.rem(lax.axis_index("seq"), 2) == 1
    same = lax.broadcasted_iota(jnp.int32, (DK, DK), 0) == lax.broadcasted_iota(jnp.int32, (DK, DK), 1)
    for h in range(mine_ref.shape[0]):
        mine, theirs = mine_ref[h], theirs_ref[h]
        total_ref[h] = joined(jnp.where(upper, theirs, mine), jnp.where(upper, mine, theirs))
        level_ref[h] = jnp.where(upper, theirs[:, :DK], jnp.zeros((DK, DK), BF16))
        after_ref[h] = jnp.where(upper, theirs[:, DK:], same.astype(BF16))


def joined(lead, trail):
    moved = dot(trail[:, DK:], lead)
    return jnp.concatenate([moved[:, :DK] + trail[:, :DK].astype(F32), moved[:, DK:]], axis=1).astype(BF16)


def two_levels(digit, four_ref, before_ref, h):
    before = before_ref[h]
    near = dot(before, four_ref[jnp.maximum(digit - 1, 0), h]).astype(BF16)
    odd = lax.rem(digit, 2) == 1
    low = jnp.where(odd, near[:, :DK], jnp.zeros((DK, DK), BF16))
    before = jnp.where(odd, near[:, DK:], before)
    first = joined(four_ref[0, h], four_ref[1, h])
    far = dot(before, first).astype(BF16)
    upper = digit >= 2
    high = jnp.where(upper, far[:, :DK], jnp.zeros((DK, DK), BF16))
    return low, high, jnp.where(upper, far[:, DK:], before), first


def quad_kernel(bit, four_ref, before_ref, total_ref, low_ref, high_ref, after_ref):
    digit = (lax.axis_index("seq") >> bit) & 3
    for h in range(before_ref.shape[0]):
        low_ref[h], high_ref[h], after_ref[h], first = two_levels(digit, four_ref, before_ref, h)
        total_ref[h] = joined(first, joined(four_ref[2, h], four_ref[3, h]))


def finish_kernel(outer, ring, core_ref, lift_ref, four_ref, before_ref, lw_ref, gate_ref, *rest):
    level_refs, keep_ref, give_ref, norm_ref = rest[:-3], rest[-3], rest[-2], rest[-1]
    digit = (lax.axis_index("seq") >> (outer - 2)) & 3
    heads = before_ref.shape[0]
    tokens = core_ref.shape[0]
    levels = lw_ref.shape[1]
    weights = lw_ref[...].reshape(heads * levels, tokens).T
    for h in range(heads):
        lanes = slice(h * DK, (h + 1) * DK)
        lifted = lift_ref[:, lanes].astype(F32)
        low, high, _, _ = two_levels(digit, four_ref, before_ref, h)
        stack = [level_ref[h] for level_ref in level_refs] + [low, high]
        scaled = []
        for b in range(outer):
            at = h * levels + levels - outer + b
            scaled.append((lifted * weights[:, at : at + 1]).astype(BF16))
        core = core_ref[:, lanes] + dot(jnp.concatenate(scaled, axis=1), jnp.concatenate(stack, axis=0))
        core = core * lax.rsqrt(jnp.mean(core * core, axis=1, keepdims=True) + EPSILON)
        gate = gate_ref[:, lanes].astype(F32)
        norm_ref[:, lanes] = (core * (gate / (1.0 + jnp.exp(-gate)))).astype(BF16)
    chunk = tokens // (2 * ring)
    pair = lax.axis_index("head") // 2
    parity = lax.rem(lax.axis_index("head"), 2)
    side = 1 - 2 * parity
    for j in range(ring):
        kept = 2 * lax.rem(pair + ring + side * (ring // 2 - j), ring) + parity
        given = 2 * lax.rem(pair + ring - side * (ring // 2 - j), ring) + 1 - parity
        rows = slice(j * chunk, (j + 1) * chunk)
        keep_ref[rows] = norm_ref[pl.ds(pl.multiple_of(kept * chunk, chunk), chunk)]
        give_ref[rows] = norm_ref[pl.ds(pl.multiple_of(given * chunk, chunk), chunk)]


def project_own_kernel(keep_ref, mine_ref, sums_ref):
    sums_ref[...] = dot(keep_ref[...], mine_ref[...])


def project_kernel(got_ref, sums_ref, direct_ref, across_ref, *out_refs):
    second = lax.rem(lax.axis_index("seq"), 2) == 1
    one, two = got_ref[:, :DK], got_ref[:, DK:]
    sums = (
        sums_ref[...]
        + dot(jnp.where(second, two, one), direct_ref[...])
        + dot(jnp.where(second, one, two), across_ref[...])
    )
    chunk = out_refs[0].shape[0]
    for j, out_ref in enumerate(out_refs):
        out_ref[...] = sums[j * chunk : (j + 1) * chunk].astype(BF16)


def call(body, out_shape, specs, flops, bytes_accessed, scratch=(), out_specs=None, mib=16):
    return pl.pallas_call(
        body,
        out_shape=out_shape,
        in_specs=specs,
        out_specs=jax.tree.map(lambda _: VMEM, out_shape) if out_specs is None else out_specs,
        scratch_shapes=scratch,
        compiler_params=pltpu.CompilerParams(vmem_limit_bytes=mib << 20),
        cost_estimate=pl.CostEstimate(flops=flops, bytes_accessed=bytes_accessed, transcendentals=0),
    )


def ring_sum(terms):
    ring = len(terms)
    half = ring // 2
    count = 2 * ring

    def hop(block, way):
        route = [(z, (z + 2 * way * (1 - 2 * (z % 2))) % count) for z in range(count)]
        return lax.ppermute(block, "head", route).astype(F32)

    ahead, behind = terms[0], terms[ring - 1]
    for t in range(1, half):
        ahead = (hop(ahead, 1) + terms[t].astype(F32)).astype(BF16)
        if t < half - 1:
            behind = (hop(behind, -1) + terms[ring - 1 - t].astype(F32)).astype(BF16)
    ahead = hop(ahead, 1) + terms[half].astype(F32)
    return (ahead + hop(behind, -1) if half > 1 else ahead).astype(BF16)


def on_device(queries, keys, values, gate, log_forget, write_rate, level_weight, w_out):
    tokens = queries.shape[0]
    heads = log_forget.shape[0]
    seq = lax.axis_size("seq")
    outer = seq.bit_length() - 1
    ring = lax.axis_size("head")
    wide = heads * DK
    pairs = [(i, i ^ 1) for i in range(ring)]

    def shape(dims, dtype=BF16):
        return jax.ShapeDtypeStruct(dims, dtype)

    sources = [pltpu.with_memory_space_constraint(x, pltpu.HBM) for x in (keys, values, log_forget, write_rate, w_out)]
    total, inner, bases, writes, rows, w_half = call(
        states_kernel,
        (
            shape((heads, DK, 2 * DK)),
            shape((heads, 4, DK, 2 * DK)),
            shape((tokens, wide), F32),
            shape((tokens, wide), F32),
            shape((8, tokens), F32),
            shape((DK, w_out.shape[1])),
        ),
        [HBM] * 5,
        2_000_000_000,
        1_000_000,
        [
            pltpu.VMEM((tokens, wide), BF16),
            pltpu.VMEM((tokens, wide), BF16),
            pltpu.VMEM((heads, tokens), F32),
            pltpu.VMEM((heads, tokens), F32),
            pltpu.SemaphoreType.DMA((4,)),
            pltpu.SemaphoreType.DMA,
        ],
        (VMEM,) * 5 + (HBM,),
    )(*sources)

    core, lifted = call(
        reads_kernel,
        (shape((tokens, wide), F32), shape((tokens, wide))),
        [VMEM] * 7,
        1_000_000_000,
        1_000_000,
    )(queries, keys, bases, writes, rows, inner, level_weight)

    cores = [(i, i ^ 1) for i in range(seq)]
    theirs = lax.ppermute(total, "seq", cores)
    direct = lax.ppermute(w_half, "head", pairs)
    matrix = shape((heads, DK, DK))
    total, level, before = call(
        merge_kernel,
        (shape((heads, DK, 2 * DK)), matrix, matrix),
        [VMEM] * 2,
        40_000_000,
        500_000,
    )(total, theirs)
    collected = [level]

    def gathered(b):
        stride = 1 << b
        groups = [[i + k * stride for k in range(4)] for i in range(seq) if (i >> b) & 3 == 0]
        return lax.all_gather(total, "seq", axis=0, axis_index_groups=groups)

    for b in range(1, outer - 2, 2):
        total, low, high, before = call(
            lambda *refs, b=b: quad_kernel(b, *refs),
            (shape((heads, DK, 2 * DK)), matrix, matrix, matrix),
            [VMEM] * 2,
            100_000_000,
            1_000_000,
        )(gathered(b), before)
        collected += [low, high]
    four = gathered(outer - 2)
    keep, give = call(
        lambda *refs: finish_kernel(outer, ring // 2, *refs),
        (shape((tokens // 2, wide)), shape((tokens // 2, wide))),
        [VMEM] * (6 + outer - 2),
        100_000_000,
        1_000_000,
        [pltpu.VMEM((tokens, wide), BF16)],
    )(core, lifted, four, before, level_weight, gate, *collected)
    give, direct = lax.optimization_barrier((give, direct))
    got = lax.ppermute(give, "head", pairs)
    across = lax.ppermute(direct, "seq", cores)
    columns = w_out.shape[1]
    step = columns // 4
    chunk = tokens // ring

    def by_columns(rows):
        return pl.BlockSpec((rows, step), lambda c: (0, c))

    whole = pl.BlockSpec((tokens // 2, wide), lambda c: (0, 0))
    sums = pl.pallas_call(
        project_own_kernel,
        grid=(columns // step,),
        out_shape=shape((tokens // 2, columns), F32),
        in_specs=[whole, by_columns(wide)],
        out_specs=by_columns(tokens // 2),
        compiler_params=pltpu.CompilerParams(vmem_limit_bytes=16 << 20),
        cost_estimate=pl.CostEstimate(flops=300_000_000, bytes_accessed=4_000_000, transcendentals=0),
    )(keep, w_out)
    terms = pl.pallas_call(
        project_kernel,
        grid=(columns // step,),
        out_shape=[shape((chunk, columns))] * (ring // 2),
        in_specs=[whole, by_columns(tokens // 2), by_columns(DK), by_columns(DK)],
        out_specs=[by_columns(chunk)] * (ring // 2),
        compiler_params=pltpu.CompilerParams(vmem_limit_bytes=16 << 20),
        cost_estimate=pl.CostEstimate(flops=300_000_000, bytes_accessed=6_000_000, transcendentals=0),
    )(got, sums, direct, across)
    return ring_sum(terms)


def solution(mesh):
    in_specs = (
        P("seq", "head"),
        P("seq", "head"),
        P("seq", "head"),
        P("seq", "head"),
        P("head", "seq"),
        P("head", "seq"),
        P("head", None, "seq"),
        P("head", None),
    )
    out_specs = P(("seq", "head"), None)
    return jax.shard_map(
        on_device, mesh=mesh, in_specs=in_specs, out_specs=out_specs, check_vma=False
    )
```

```python
import jax
import jax.numpy as jnp
from jax import lax
from jax.experimental import pallas as pl
from jax.experimental.pallas import tpu as pltpu
from jax.sharding import PartitionSpec as P

DK = 128
BLOCK = 64
TILE = 128
EPSILON = 1e-06
F32 = jnp.float32
BF16 = jnp.bfloat16
VMEM = pl.BlockSpec(memory_space=pltpu.VMEM)
HBM = pl.BlockSpec(memory_space=pltpu.HBM)


def dot(left, right, dims=((1,), (0,)), precision=None):
    return lax.dot_general(left, right, (dims, ((), ())), precision=precision, preferred_element_type=F32)


def halves(matrix):
    high = matrix.astype(BF16)
    return high, (matrix - high.astype(F32)).astype(BF16)


def paired(matrix):
    return jnp.concatenate(halves(matrix), axis=1)


def twice(matrix):
    return jnp.concatenate([matrix, matrix], axis=0)


def product(left, right):
    wide = dot(left, twice(right))
    return wide[:, :DK] + wide[:, DK:]


def tile_masks():
    row = lax.broadcasted_iota(jnp.int32, (TILE, TILE), 0)
    col = lax.broadcasted_iota(jnp.int32, (TILE, TILE), 1)
    return row, col, row // BLOCK == col // BLOCK


def states_kernel(
    k_in, v_in, lf_in, wr_in, full_ref, x_ref, y_ref, w_ref, u_ref, rows_ref, half_ref,
    k_ref, v_ref, lf_ref, wr_ref, in_sems, half_sem,
):
    copies = [
        pltpu.make_async_copy(source, target, in_sems.at[i])
        for i, (source, target) in enumerate(((k_in, k_ref), (lf_in, lf_ref), (wr_in, wr_ref), (v_in, v_ref)))
    ]
    for copy in copies:
        copy.start()
    count = half_ref.shape[0]
    first = pl.multiple_of(lax.rem(lax.axis_index("seq"), 2) * count, count)
    half = pltpu.make_async_copy(full_ref.at[pl.ds(first, count)], half_ref, half_sem)
    half.start()
    for copy in copies:
        copy.wait()
    tokens = k_ref.shape[0]
    heads = lf_ref.shape[0]
    tiles = tokens // TILE
    row, col, same = tile_masks()
    inclusive = same & (row >= col)
    strict = same & (row > col)
    eye = (row == col).astype(F32)

    def by_tile(ref):
        return jnp.concatenate([ref[:, t * TILE : (t + 1) * TILE] for t in range(tiles)], axis=0)

    log_forget, rate = by_tile(lf_ref), by_tile(wr_ref)
    exact = lax.Precision.HIGHEST
    cum = dot(log_forget, inclusive.astype(F32), ((1,), (1,)), exact)
    total = dot(log_forget, same.astype(F32), ((1,), (1,)), exact)
    count = tiles * heads
    pad = jnp.zeros((16 - 3 * count, TILE), F32)
    columns = jnp.concatenate([cum, total, rate, pad], axis=0).T
    units = [(t, h) for t in range(tiles) for h in range(heads)]
    lowers, keys, norms, inverses = [], [], [], []
    for n, (t, h) in enumerate(units):
        key = k_ref[t * TILE : (t + 1) * TILE, h * DK : (h + 1) * DK]
        key_f = key.astype(F32)
        key_key = dot(key, key, ((1,), (1,)))
        inv_col = lax.rsqrt(jnp.sum(key_f * key_f, axis=1, keepdims=True) + EPSILON)
        inv_row = lax.rsqrt(jnp.sum(key_key * eye, axis=0, keepdims=True) + EPSILON)
        rate_col = columns[:, 2 * count + n : 2 * count + n + 1]
        lower = jnp.where(strict, key_key * (rate_col * inv_col) * inv_row, 0.0)
        inverses.append(eye - jnp.where(row // 2 == col // 2, lower, 0.0))
        lowers.append(paired(lower))
        keys.append((key, key_f))
        norms.append((inv_col, inv_row))
    width = 2
    while width < BLOCK:
        band = ((row // width != col // width) & (row // (2 * width) == col // (2 * width))).astype(F32).astype(BF16)
        band = jnp.concatenate([band, band], axis=1)
        split = [paired(inverse) for inverse in inverses]
        inner = [product(lowers[n] * band, split[n]) for n in range(count)]
        inverses = [inverses[n] - product(split[n], paired(inner[n])) for n in range(count)]
        width *= 2
    blocks = tokens // BLOCK
    leaf = {}
    for n, (t, h) in enumerate(units):
        rows = slice(t * TILE, (t + 1) * TILE)
        lanes = slice(h * DK, (h + 1) * DK)
        key, key_f = keys[n]
        inv_col, inv_row = norms[n]
        cum_col = columns[:, n : n + 1]
        total_col = columns[:, count + n : count + n + 1]
        fading = jnp.exp(jnp.where(inclusive, cum_col - cum[n : n + 1], -1e30))
        solved = inverses[n] * rate[n : n + 1]
        bases = dot(paired(solved * inv_row), twice(key))
        writes = dot(paired(solved * fading), twice(v_ref[rows, lanes]))
        w_ref[rows, lanes] = bases
        u_ref[rows, lanes] = writes
        both = jnp.concatenate([writes * (jnp.exp(total_col - cum_col) * inv_col), bases * inv_col], axis=1)
        turned = key_f.T
        picked = [jnp.where(col // BLOCK == b, turned, 0.0).astype(BF16) for b in range(TILE // BLOCK)]
        picked = jnp.concatenate([jnp.concatenate([p, p], axis=1) for p in picked], axis=0)
        raw = dot(picked, jnp.concatenate(halves(both), axis=0))
        for b in range(TILE // BLOCK):
            part = raw[b * DK : (b + 1) * DK]
            fade = jnp.exp(total[n : n + 1, b * BLOCK : b * BLOCK + 1])
            leaf[h, t * (TILE // BLOCK) + b] = part[:, :DK], fade * (eye - part[:, DK:])

    def merge(lead, trail):
        moved = dot(trail[1].astype(BF16), jnp.concatenate(lead, axis=1).astype(BF16))
        return moved[:, :DK] + trail[0], moved[:, DK:]

    def stored(state):
        return jnp.concatenate(state, axis=1).astype(BF16)

    firsts = [merge(leaf[h, 0], leaf[h, 1]) for h in range(heads)]
    seconds = [merge(leaf[h, 2], leaf[h, 3]) for h in range(heads)]
    for h in range(heads):
        x_ref[h] = stored(merge(firsts[h], seconds[h]))
    for h in range(heads):
        y_ref[h, 0] = stored(leaf[h, 0])
        y_ref[h, 1] = stored(firsts[h])
        y_ref[h, 2] = dot(leaf[h, 2][1].astype(BF16), stored(firsts[h])).astype(BF16)
        y_ref[h, 3] = stored(leaf[h, 2])
    filler = jnp.zeros((8 - 2 * heads, TILE), F32)
    for t in range(tiles):
        found = [norms[t * heads + h][1] for h in range(heads)]
        rows_ref[:, t * TILE : (t + 1) * TILE] = jnp.concatenate(
            [cum[t * heads : (t + 1) * heads]] + found + [filler], axis=0
        )
    half.wait()


def reads_kernel(q_ref, k_ref, w_ref, u_ref, rows_ref, y_ref, lw_ref, core_ref, lift_ref):
    tokens = k_ref.shape[0]
    heads = y_ref.shape[0]
    row, col, same = tile_masks()
    inclusive = same & (row >= col)
    rows = rows_ref[...]
    columns = rows.T
    levels = lw_ref.shape[1]
    weights = lw_ref[...].reshape(heads * levels, tokens).T
    for h in range(heads):
        lanes = slice(h * DK, (h + 1) * DK)

        def weight(level, span):
            at = h * levels + level
            return weights[span, at : at + 1]

        owns, reaches = [], []
        for t in range(tokens // TILE):
            here = slice(t * TILE, (t + 1) * TILE)
            query = q_ref[here, lanes]
            query_f = query.astype(F32)
            inv_query = lax.rsqrt(jnp.sum(query_f * query_f, axis=1, keepdims=True) + EPSILON)
            query_key = dot(query, k_ref[here, lanes], ((1,), (1,))) * inv_query * rows[heads + h : heads + h + 1, here]
            cum_col = columns[here, h : h + 1]
            fading = jnp.exp(jnp.where(inclusive, cum_col - rows[h : h + 1, here], -1e30))
            owns.append(product(paired(query_key * fading), paired(u_ref[here, lanes])))
            masked = jnp.where(inclusive, query_key, 0.0)
            reach = query_f * inv_query - product(paired(masked), paired(w_ref[here, lanes]))
            reaches.append((jnp.exp(cum_col) * reach).astype(BF16))
        spans = [slice(g * BLOCK, (g + 1) * BLOCK) for g in range(4)]
        own = [owns[g // 2][spans[g % 2]] for g in range(4)]
        reach = [reaches[g // 2][spans[g % 2]] for g in range(4)]
        read1 = dot(reach[1], y_ref[h, 0])
        read2 = dot(reach[2], y_ref[h, 1])
        read3 = dot(reach[3], y_ref[h, 2])
        near3 = dot(reach[3], y_ref[h, 3, :, :DK])
        core_ref[spans[0], lanes] = weight(0, spans[0]) * own[0]
        core_ref[spans[1], lanes] = weight(0, spans[1]) * own[1] + weight(1, spans[1]) * read1[:, :DK]
        core_ref[spans[2], lanes] = weight(0, spans[2]) * own[2] + weight(2, spans[2]) * read2[:, :DK]
        core_ref[spans[3], lanes] = (
            weight(0, spans[3]) * own[3] + weight(1, spans[3]) * near3 + weight(2, spans[3]) * read3[:, :DK]
        )
        lift_ref[spans[0], lanes] = reach[0]
        lift_ref[spans[1], lanes] = read1[:, DK:].astype(BF16)
        lift_ref[spans[2], lanes] = read2[:, DK:].astype(BF16)
        lift_ref[spans[3], lanes] = read3[:, DK:].astype(BF16)


def merge_kernel(mine_ref, theirs_ref, total_ref, level_ref, after_ref):
    upper = lax.rem(lax.axis_index("seq"), 2) == 1
    same = lax.broadcasted_iota(jnp.int32, (DK, DK), 0) == lax.broadcasted_iota(jnp.int32, (DK, DK), 1)
    for h in range(mine_ref.shape[0]):
        mine, theirs = mine_ref[h], theirs_ref[h]
        total_ref[h] = joined(jnp.where(upper, theirs, mine), jnp.where(upper, mine, theirs))
        level_ref[h] = jnp.where(upper, theirs[:, :DK], jnp.zeros((DK, DK), BF16))
        after_ref[h] = jnp.where(upper, theirs[:, DK:], same.astype(BF16))


def joined(lead, trail):
    moved = dot(trail[:, DK:], lead)
    return jnp.concatenate([moved[:, :DK] + trail[:, :DK].astype(F32), moved[:, DK:]], axis=1).astype(BF16)


def two_levels(digit, four_ref, before_ref, h):
    before = before_ref[h]
    near = dot(before, four_ref[jnp.maximum(digit - 1, 0), h]).astype(BF16)
    odd = lax.rem(digit, 2) == 1
    low = jnp.where(odd, near[:, :DK], jnp.zeros((DK, DK), BF16))
    before = jnp.where(odd, near[:, DK:], before)
    first = joined(four_ref[0, h], four_ref[1, h])
    far = dot(before, first).astype(BF16)
    upper = digit >= 2
    high = jnp.where(upper, far[:, :DK], jnp.zeros((DK, DK), BF16))
    return low, high, jnp.where(upper, far[:, DK:], before), first


def quad_kernel(bit, four_ref, before_ref, total_ref, low_ref, high_ref, after_ref):
    digit = (lax.axis_index("seq") >> bit) & 3
    for h in range(before_ref.shape[0]):
        low_ref[h], high_ref[h], after_ref[h], first = two_levels(digit, four_ref, before_ref, h)
        total_ref[h] = joined(first, joined(four_ref[2, h], four_ref[3, h]))


def finish_kernel(outer, ring, core_ref, lift_ref, four_ref, before_ref, lw_ref, gate_ref, *rest):
    level_refs, keep_ref, give_ref, norm_ref = rest[:-3], rest[-3], rest[-2], rest[-1]
    digit = (lax.axis_index("seq") >> (outer - 2)) & 3
    heads = before_ref.shape[0]
    tokens = core_ref.shape[0]
    levels = lw_ref.shape[1]
    weights = lw_ref[...].reshape(heads * levels, tokens).T
    for h in range(heads):
        lanes = slice(h * DK, (h + 1) * DK)
        lifted = lift_ref[:, lanes].astype(F32)
        low, high, _, _ = two_levels(digit, four_ref, before_ref, h)
        stack = [level_ref[h] for level_ref in level_refs] + [low, high]
        scaled = []
        for b in range(outer):
            at = h * levels + levels - outer + b
            scaled.append((lifted * weights[:, at : at + 1]).astype(BF16))
        core = core_ref[:, lanes] + dot(jnp.concatenate(scaled, axis=1), jnp.concatenate(stack, axis=0))
        core = core * lax.rsqrt(jnp.mean(core * core, axis=1, keepdims=True) + EPSILON)
        gate = gate_ref[:, lanes].astype(F32)
        norm_ref[:, lanes] = (core * (gate / (1.0 + jnp.exp(-gate)))).astype(BF16)
    chunk = tokens // (2 * ring)
    pair = lax.axis_index("head") // 2
    parity = lax.rem(lax.axis_index("head"), 2)
    side = 1 - 2 * lax.rem(lax.axis_index("head") + lax.axis_index("seq"), 2)
    for j in range(ring):
        kept = 2 * lax.rem(pair + ring + side * (ring // 2 - j), ring) + parity
        given = 2 * lax.rem(pair + ring - side * (ring // 2 - j), ring) + 1 - parity
        rows = slice(j * chunk, (j + 1) * chunk)
        keep_ref[rows] = norm_ref[pl.ds(pl.multiple_of(kept * chunk, chunk), chunk)]
        give_ref[rows] = norm_ref[pl.ds(pl.multiple_of(given * chunk, chunk), chunk)]


def project_own_kernel(keep_ref, mine_ref, sums_ref):
    sums_ref[...] = dot(keep_ref[...], mine_ref[...])


def project_kernel(got_ref, sums_ref, direct_ref, across_ref, *out_refs):
    second = lax.rem(lax.axis_index("seq"), 2) == 1
    one, two = got_ref[:, :DK], got_ref[:, DK:]
    sums = (
        sums_ref[...]
        + dot(jnp.where(second, two, one), direct_ref[...])
        + dot(jnp.where(second, one, two), across_ref[...])
    )
    chunk = out_refs[0].shape[0]
    for j, out_ref in enumerate(out_refs):
        out_ref[...] = sums[j * chunk : (j + 1) * chunk].astype(BF16)


def call(body, out_shape, specs, flops, bytes_accessed, scratch=(), out_specs=None, mib=16):
    return pl.pallas_call(
        body,
        out_shape=out_shape,
        in_specs=specs,
        out_specs=jax.tree.map(lambda _: VMEM, out_shape) if out_specs is None else out_specs,
        scratch_shapes=scratch,
        compiler_params=pltpu.CompilerParams(vmem_limit_bytes=mib << 20),
        cost_estimate=pl.CostEstimate(flops=flops, bytes_accessed=bytes_accessed, transcendentals=0),
    )


def ring_sum(terms):
    ring = len(terms)
    half = ring // 2
    count = 2 * ring
    slabs = lax.axis_size("seq")

    def hop(block, way):
        route = []
        for s in range(slabs):
            for z in range(count):
                step = 2 * way * (1 - 2 * ((s + z) % 2))
                route.append((s * count + z, s * count + (z + step) % count))
        return lax.ppermute(block, ("seq", "head"), route).astype(F32)

    ahead, behind = terms[0], terms[ring - 1]
    for t in range(1, half):
        ahead = (hop(ahead, 1) + terms[t].astype(F32)).astype(BF16)
        if t < half - 1:
            behind = (hop(behind, -1) + terms[ring - 1 - t].astype(F32)).astype(BF16)
    ahead = hop(ahead, 1) + terms[half].astype(F32)
    return (ahead + hop(behind, -1) if half > 1 else ahead).astype(BF16)


def on_device(queries, keys, values, gate, log_forget, write_rate, level_weight, w_out):
    tokens = queries.shape[0]
    heads = log_forget.shape[0]
    seq = lax.axis_size("seq")
    outer = seq.bit_length() - 1
    ring = lax.axis_size("head")
    wide = heads * DK
    pairs = [(i, i ^ 1) for i in range(ring)]

    def shape(dims, dtype=BF16):
        return jax.ShapeDtypeStruct(dims, dtype)

    sources = [pltpu.with_memory_space_constraint(x, pltpu.HBM) for x in (keys, values, log_forget, write_rate, w_out)]
    total, inner, bases, writes, rows, w_half = call(
        states_kernel,
        (
            shape((heads, DK, 2 * DK)),
            shape((heads, 4, DK, 2 * DK)),
            shape((tokens, wide), F32),
            shape((tokens, wide), F32),
            shape((8, tokens), F32),
            shape((DK, w_out.shape[1])),
        ),
        [HBM] * 5,
        2_000_000_000,
        1_000_000,
        [
            pltpu.VMEM((tokens, wide), BF16),
            pltpu.VMEM((tokens, wide), BF16),
            pltpu.VMEM((heads, tokens), F32),
            pltpu.VMEM((heads, tokens), F32),
            pltpu.SemaphoreType.DMA((4,)),
            pltpu.SemaphoreType.DMA,
        ],
        (VMEM,) * 5 + (HBM,),
    )(*sources)

    core, lifted = call(
        reads_kernel,
        (shape((tokens, wide), F32), shape((tokens, wide))),
        [VMEM] * 7,
        1_000_000_000,
        1_000_000,
    )(queries, keys, bases, writes, rows, inner, level_weight)

    cores = [(i, i ^ 1) for i in range(seq)]
    theirs = lax.ppermute(total, "seq", cores)
    direct = lax.ppermute(w_half, "head", pairs)
    matrix = shape((heads, DK, DK))
    total, level, before = call(
        merge_kernel,
        (shape((heads, DK, 2 * DK)), matrix, matrix),
        [VMEM] * 2,
        40_000_000,
        500_000,
    )(total, theirs)
    collected = [level]

    def gathered(b):
        stride = 1 << b
        groups = [[i + k * stride for k in range(4)] for i in range(seq) if (i >> b) & 3 == 0]
        return lax.all_gather(total, "seq", axis=0, axis_index_groups=groups)

    for b in range(1, outer - 2, 2):
        total, low, high, before = call(
            lambda *refs, b=b: quad_kernel(b, *refs),
            (shape((heads, DK, 2 * DK)), matrix, matrix, matrix),
            [VMEM] * 2,
            100_000_000,
            1_000_000,
        )(gathered(b), before)
        collected += [low, high]
    four = gathered(outer - 2)
    keep, give = call(
        lambda *refs: finish_kernel(outer, ring // 2, *refs),
        (shape((tokens // 2, wide)), shape((tokens // 2, wide))),
        [VMEM] * (6 + outer - 2),
        100_000_000,
        1_000_000,
        [pltpu.VMEM((tokens, wide), BF16)],
    )(core, lifted, four, before, level_weight, gate, *collected)
    give, direct = lax.optimization_barrier((give, direct))
    got = lax.ppermute(give, "head", pairs)
    across = lax.ppermute(direct, "seq", cores)
    columns = w_out.shape[1]
    step = columns // 4
    chunk = tokens // ring

    def by_columns(rows):
        return pl.BlockSpec((rows, step), lambda c: (0, c))

    whole = pl.BlockSpec((tokens // 2, wide), lambda c: (0, 0))
    sums = pl.pallas_call(
        project_own_kernel,
        grid=(columns // step,),
        out_shape=shape((tokens // 2, columns), F32),
        in_specs=[whole, by_columns(wide)],
        out_specs=by_columns(tokens // 2),
        compiler_params=pltpu.CompilerParams(vmem_limit_bytes=16 << 20),
        cost_estimate=pl.CostEstimate(flops=300_000_000, bytes_accessed=4_000_000, transcendentals=0),
    )(keep, w_out)
    terms = pl.pallas_call(
        project_kernel,
        grid=(columns // step,),
        out_shape=[shape((chunk, columns))] * (ring // 2),
        in_specs=[whole, by_columns(tokens // 2), by_columns(DK), by_columns(DK)],
        out_specs=[by_columns(chunk)] * (ring // 2),
        compiler_params=pltpu.CompilerParams(vmem_limit_bytes=16 << 20),
        cost_estimate=pl.CostEstimate(flops=300_000_000, bytes_accessed=6_000_000, transcendentals=0),
    )(got, sums, direct, across)
    return ring_sum(terms)


def solution(mesh):
    in_specs = (
        P("seq", "head"),
        P("seq", "head"),
        P("seq", "head"),
        P("seq", "head"),
        P("head", "seq"),
        P("head", "seq"),
        P("head", None, "seq"),
        P("head", None),
    )
    out_specs = P(("seq", "head"), None)
    return jax.shard_map(
        on_device, mesh=mesh, in_specs=in_specs, out_specs=out_specs, check_vma=False
    )
```

```python
import jax
import jax.numpy as jnp
from jax import lax
from jax.experimental import pallas as pl
from jax.experimental.pallas import tpu as pltpu
from jax.sharding import PartitionSpec as P

DK = 128
BLOCK = 64
TILE = 128
EPSILON = 1e-06
F32 = jnp.float32
BF16 = jnp.bfloat16
VMEM = pl.BlockSpec(memory_space=pltpu.VMEM)
HBM = pl.BlockSpec(memory_space=pltpu.HBM)


def dot(left, right, dims=((1,), (0,)), precision=None):
    return lax.dot_general(left, right, (dims, ((), ())), precision=precision, preferred_element_type=F32)


def halves(matrix):
    high = matrix.astype(BF16)
    return high, (matrix - high.astype(F32)).astype(BF16)


def paired(matrix):
    return jnp.concatenate(halves(matrix), axis=1)


def twice(matrix):
    return jnp.concatenate([matrix, matrix], axis=0)


def product(left, right):
    wide = dot(left, twice(right))
    return wide[:, :DK] + wide[:, DK:]


def tile_masks():
    row = lax.broadcasted_iota(jnp.int32, (TILE, TILE), 0)
    col = lax.broadcasted_iota(jnp.int32, (TILE, TILE), 1)
    return row, col, row // BLOCK == col // BLOCK


def states_kernel(
    k_in, v_in, lf_in, wr_in, full_ref, x_ref, y_ref, w_ref, u_ref, rows_ref, half_ref,
    k_ref, v_ref, lf_ref, wr_ref, in_sems, half_sem,
):
    copies = [
        pltpu.make_async_copy(source, target, in_sems.at[i])
        for i, (source, target) in enumerate(((k_in, k_ref), (lf_in, lf_ref), (wr_in, wr_ref), (v_in, v_ref)))
    ]
    for copy in copies:
        copy.start()
    count = half_ref.shape[0]
    first = pl.multiple_of(lax.rem(lax.axis_index("seq"), 2) * count, count)
    half = pltpu.make_async_copy(full_ref.at[pl.ds(first, count)], half_ref, half_sem)
    half.start()
    for copy in copies:
        copy.wait()
    tokens = k_ref.shape[0]
    heads = lf_ref.shape[0]
    tiles = tokens // TILE
    row, col, same = tile_masks()
    inclusive = same & (row >= col)
    strict = same & (row > col)
    eye = (row == col).astype(F32)

    def by_tile(ref):
        return jnp.concatenate([ref[:, t * TILE : (t + 1) * TILE] for t in range(tiles)], axis=0)

    log_forget, rate = by_tile(lf_ref), by_tile(wr_ref)
    exact = lax.Precision.HIGHEST
    cum = dot(log_forget, inclusive.astype(F32), ((1,), (1,)), exact)
    total = dot(log_forget, same.astype(F32), ((1,), (1,)), exact)
    count = tiles * heads
    pad = jnp.zeros((16 - 3 * count, TILE), F32)
    columns = jnp.concatenate([cum, total, rate, pad], axis=0).T
    units = [(t, h) for t in range(tiles) for h in range(heads)]
    lowers, keys, norms, inverses = [], [], [], []
    for n, (t, h) in enumerate(units):
        key = k_ref[t * TILE : (t + 1) * TILE, h * DK : (h + 1) * DK]
        key_f = key.astype(F32)
        key_key = dot(key, key, ((1,), (1,)))
        inv_col = lax.rsqrt(jnp.sum(key_f * key_f, axis=1, keepdims=True) + EPSILON)
        inv_row = lax.rsqrt(jnp.sum(key_key * eye, axis=0, keepdims=True) + EPSILON)
        rate_col = columns[:, 2 * count + n : 2 * count + n + 1]
        lower = jnp.where(strict, key_key * (rate_col * inv_col) * inv_row, 0.0)
        inverses.append(eye - jnp.where(row // 2 == col // 2, lower, 0.0))
        lowers.append(paired(lower))
        keys.append((key, key_f))
        norms.append((inv_col, inv_row))
    width = 2
    while width < BLOCK:
        band = ((row // width != col // width) & (row // (2 * width) == col // (2 * width))).astype(F32).astype(BF16)
        band = jnp.concatenate([band, band], axis=1)
        split = [paired(inverse) for inverse in inverses]
        inner = [product(lowers[n] * band, split[n]) for n in range(count)]
        inverses = [inverses[n] - product(split[n], paired(inner[n])) for n in range(count)]
        width *= 2
    blocks = tokens // BLOCK
    leaf = {}
    for n, (t, h) in enumerate(units):
        rows = slice(t * TILE, (t + 1) * TILE)
        lanes = slice(h * DK, (h + 1) * DK)
        key, key_f = keys[n]
        inv_col, inv_row = norms[n]
        cum_col = columns[:, n : n + 1]
        total_col = columns[:, count + n : count + n + 1]
        fading = jnp.exp(jnp.where(inclusive, cum_col - cum[n : n + 1], -1e30))
        solved = inverses[n] * rate[n : n + 1]
        bases = dot(paired(solved * inv_row), twice(key))
        writes = dot(paired(solved * fading), twice(v_ref[rows, lanes]))
        w_ref[rows, lanes] = bases
        u_ref[rows, lanes] = writes
        both = jnp.concatenate([writes * (jnp.exp(total_col - cum_col) * inv_col), bases * inv_col], axis=1)
        turned = key_f.T
        picked = [jnp.where(col // BLOCK == b, turned, 0.0).astype(BF16) for b in range(TILE // BLOCK)]
        picked = jnp.concatenate([jnp.concatenate([p, p], axis=1) for p in picked], axis=0)
        raw = dot(picked, jnp.concatenate(halves(both), axis=0))
        for b in range(TILE // BLOCK):
            part = raw[b * DK : (b + 1) * DK]
            fade = jnp.exp(total[n : n + 1, b * BLOCK : b * BLOCK + 1])
            leaf[h, t * (TILE // BLOCK) + b] = part[:, :DK], fade * (eye - part[:, DK:])

    def merge(lead, trail):
        moved = dot(trail[1].astype(BF16), jnp.concatenate(lead, axis=1).astype(BF16))
        return moved[:, :DK] + trail[0], moved[:, DK:]

    def stored(state):
        return jnp.concatenate(state, axis=1).astype(BF16)

    firsts = [merge(leaf[h, 0], leaf[h, 1]) for h in range(heads)]
    seconds = [merge(leaf[h, 2], leaf[h, 3]) for h in range(heads)]
    for h in range(heads):
        x_ref[h] = stored(merge(firsts[h], seconds[h]))
    for h in range(heads):
        y_ref[h, 0] = stored(leaf[h, 0])
        y_ref[h, 1] = stored(firsts[h])
        y_ref[h, 2] = dot(leaf[h, 2][1].astype(BF16), stored(firsts[h])).astype(BF16)
        y_ref[h, 3] = stored(leaf[h, 2])
    filler = jnp.zeros((8 - 2 * heads, TILE), F32)
    for t in range(tiles):
        found = [norms[t * heads + h][1] for h in range(heads)]
        rows_ref[:, t * TILE : (t + 1) * TILE] = jnp.concatenate(
            [cum[t * heads : (t + 1) * heads]] + found + [filler], axis=0
        )
    half.wait()


def reads_kernel(q_ref, k_ref, w_ref, u_ref, rows_ref, y_ref, lw_ref, core_ref, lift_ref):
    tokens = k_ref.shape[0]
    heads = y_ref.shape[0]
    row, col, same = tile_masks()
    inclusive = same & (row >= col)
    rows = rows_ref[...]
    columns = rows.T
    levels = lw_ref.shape[1]
    weights = lw_ref[...].reshape(heads * levels, tokens).T
    for h in range(heads):
        lanes = slice(h * DK, (h + 1) * DK)

        def weight(level, span):
            at = h * levels + level
            return weights[span, at : at + 1]

        owns, reaches = [], []
        for t in range(tokens // TILE):
            here = slice(t * TILE, (t + 1) * TILE)
            query = q_ref[here, lanes]
            query_f = query.astype(F32)
            inv_query = lax.rsqrt(jnp.sum(query_f * query_f, axis=1, keepdims=True) + EPSILON)
            query_key = dot(query, k_ref[here, lanes], ((1,), (1,))) * inv_query * rows[heads + h : heads + h + 1, here]
            cum_col = columns[here, h : h + 1]
            fading = jnp.exp(jnp.where(inclusive, cum_col - rows[h : h + 1, here], -1e30))
            owns.append(product(paired(query_key * fading), paired(u_ref[here, lanes])))
            masked = jnp.where(inclusive, query_key, 0.0)
            reach = query_f * inv_query - product(paired(masked), paired(w_ref[here, lanes]))
            reaches.append((jnp.exp(cum_col) * reach).astype(BF16))
        spans = [slice(g * BLOCK, (g + 1) * BLOCK) for g in range(4)]
        own = [owns[g // 2][spans[g % 2]] for g in range(4)]
        reach = [reaches[g // 2][spans[g % 2]] for g in range(4)]
        read1 = dot(reach[1], y_ref[h, 0])
        read2 = dot(reach[2], y_ref[h, 1])
        read3 = dot(reach[3], y_ref[h, 2])
        near3 = dot(reach[3], y_ref[h, 3, :, :DK])
        core_ref[spans[0], lanes] = weight(0, spans[0]) * own[0]
        core_ref[spans[1], lanes] = weight(0, spans[1]) * own[1] + weight(1, spans[1]) * read1[:, :DK]
        core_ref[spans[2], lanes] = weight(0, spans[2]) * own[2] + weight(2, spans[2]) * read2[:, :DK]
        core_ref[spans[3], lanes] = (
            weight(0, spans[3]) * own[3] + weight(1, spans[3]) * near3 + weight(2, spans[3]) * read3[:, :DK]
        )
        lift_ref[spans[0], lanes] = reach[0]
        lift_ref[spans[1], lanes] = read1[:, DK:].astype(BF16)
        lift_ref[spans[2], lanes] = read2[:, DK:].astype(BF16)
        lift_ref[spans[3], lanes] = read3[:, DK:].astype(BF16)


def merge_kernel(mine_ref, theirs_ref, total_ref, level_ref, after_ref):
    upper = lax.rem(lax.axis_index("seq"), 2) == 1
    same = lax.broadcasted_iota(jnp.int32, (DK, DK), 0) == lax.broadcasted_iota(jnp.int32, (DK, DK), 1)
    for h in range(mine_ref.shape[0]):
        mine, theirs = mine_ref[h], theirs_ref[h]
        total_ref[h] = joined(jnp.where(upper, theirs, mine), jnp.where(upper, mine, theirs))
        level_ref[h] = jnp.where(upper, theirs[:, :DK], jnp.zeros((DK, DK), BF16))
        after_ref[h] = jnp.where(upper, theirs[:, DK:], same.astype(BF16))


def joined(lead, trail):
    moved = dot(trail[:, DK:], lead)
    return jnp.concatenate([moved[:, :DK] + trail[:, :DK].astype(F32), moved[:, DK:]], axis=1).astype(BF16)


def two_levels(digit, four_ref, before_ref, h):
    before = before_ref[h]
    near = dot(before, four_ref[jnp.maximum(digit - 1, 0), h]).astype(BF16)
    odd = lax.rem(digit, 2) == 1
    low = jnp.where(odd, near[:, :DK], jnp.zeros((DK, DK), BF16))
    before = jnp.where(odd, near[:, DK:], before)
    first = joined(four_ref[0, h], four_ref[1, h])
    far = dot(before, first).astype(BF16)
    upper = digit >= 2
    high = jnp.where(upper, far[:, :DK], jnp.zeros((DK, DK), BF16))
    return low, high, jnp.where(upper, far[:, DK:], before), first


def quad_kernel(bit, four_ref, before_ref, total_ref, low_ref, high_ref, after_ref):
    digit = (lax.axis_index("seq") >> bit) & 3
    for h in range(before_ref.shape[0]):
        low_ref[h], high_ref[h], after_ref[h], first = two_levels(digit, four_ref, before_ref, h)
        total_ref[h] = joined(first, joined(four_ref[2, h], four_ref[3, h]))


def hop_order(ring):
    return [0, ring - 1] + list(range(1, ring - 1))


def finish_kernel(outer, ring, core_ref, lift_ref, four_ref, before_ref, lw_ref, gate_ref, *rest):
    level_refs, keep_ref, give_ref, norm_ref = rest[:-3], rest[-3], rest[-2], rest[-1]
    digit = (lax.axis_index("seq") >> (outer - 2)) & 3
    heads = before_ref.shape[0]
    tokens = core_ref.shape[0]
    levels = lw_ref.shape[1]
    weights = lw_ref[...].reshape(heads * levels, tokens).T
    for h in range(heads):
        lanes = slice(h * DK, (h + 1) * DK)
        lifted = lift_ref[:, lanes].astype(F32)
        low, high, _, _ = two_levels(digit, four_ref, before_ref, h)
        stack = [level_ref[h] for level_ref in level_refs] + [low, high]
        scaled = []
        for b in range(outer):
            at = h * levels + levels - outer + b
            scaled.append((lifted * weights[:, at : at + 1]).astype(BF16))
        core = core_ref[:, lanes] + dot(jnp.concatenate(scaled, axis=1), jnp.concatenate(stack, axis=0))
        core = core * lax.rsqrt(jnp.mean(core * core, axis=1, keepdims=True) + EPSILON)
        gate = gate_ref[:, lanes].astype(F32)
        norm_ref[:, lanes] = (core * (gate / (1.0 + jnp.exp(-gate)))).astype(BF16)
    chunk = tokens // (2 * ring)
    pair = lax.axis_index("head") // 2
    parity = lax.rem(lax.axis_index("head"), 2)
    side = 1 - 2 * lax.rem(lax.axis_index("head") + lax.axis_index("seq"), 2)
    for n, j in enumerate(hop_order(ring)):
        kept = 2 * lax.rem(pair + ring + side * (ring // 2 - j), ring) + parity
        given = 2 * lax.rem(pair + ring - side * (ring // 2 - j), ring) + 1 - parity
        rows = slice(n * chunk, (n + 1) * chunk)
        keep_ref[rows] = norm_ref[pl.ds(pl.multiple_of(kept * chunk, chunk), chunk)]
        give_ref[rows] = norm_ref[pl.ds(pl.multiple_of(given * chunk, chunk), chunk)]


def project_own_kernel(keep_ref, mine_ref, sums_ref):
    sums_ref[...] = dot(keep_ref[...], mine_ref[...])


def project_direct_kernel(got_ref, sums_ref, direct_ref, first_ref, others_ref):
    second = lax.rem(lax.axis_index("seq"), 2) == 1
    sums = sums_ref[...] + dot(jnp.where(second, got_ref[:, DK:], got_ref[:, :DK]), direct_ref[...])
    count = first_ref.shape[0]
    first_ref[...] = sums[:count]
    others_ref[...] = sums[count:]


def project_kernel(start, got_ref, sums_ref, across_ref, *out_refs):
    second = lax.rem(lax.axis_index("seq"), 2) == 1
    rows = slice(start, start + sums_ref.shape[0])
    sums = sums_ref[...] + dot(jnp.where(second, got_ref[rows, :DK], got_ref[rows, DK:]), across_ref[...])
    chunk = out_refs[0].shape[0]
    for j, out_ref in enumerate(out_refs):
        out_ref[...] = sums[j * chunk : (j + 1) * chunk].astype(BF16)


def call(body, out_shape, specs, flops, bytes_accessed, scratch=(), out_specs=None, mib=16):
    return pl.pallas_call(
        body,
        out_shape=out_shape,
        in_specs=specs,
        out_specs=jax.tree.map(lambda _: VMEM, out_shape) if out_specs is None else out_specs,
        scratch_shapes=scratch,
        compiler_params=pltpu.CompilerParams(vmem_limit_bytes=mib << 20),
        cost_estimate=pl.CostEstimate(flops=flops, bytes_accessed=bytes_accessed, transcendentals=0),
    )


def ring_sum(terms):
    ring = len(terms)
    half = ring // 2
    count = 2 * ring
    slabs = lax.axis_size("seq")

    def hop(block, way):
        route = []
        for s in range(slabs):
            for z in range(count):
                step = 2 * way * (1 - 2 * ((s + z) % 2))
                route.append((s * count + z, s * count + (z + step) % count))
        return lax.ppermute(block, ("seq", "head"), route).astype(F32)

    ahead, behind = terms[0], terms[ring - 1]
    for t in range(1, half):
        ahead = (hop(ahead, 1) + terms[t].astype(F32)).astype(BF16)
        if t < half - 1:
            behind = (hop(behind, -1) + terms[ring - 1 - t].astype(F32)).astype(BF16)
    ahead = hop(ahead, 1) + terms[half].astype(F32)
    return (ahead + hop(behind, -1) if half > 1 else ahead).astype(BF16)


def on_device(queries, keys, values, gate, log_forget, write_rate, level_weight, w_out):
    tokens = queries.shape[0]
    heads = log_forget.shape[0]
    seq = lax.axis_size("seq")
    outer = seq.bit_length() - 1
    ring = lax.axis_size("head")
    wide = heads * DK
    pairs = [(i, i ^ 1) for i in range(ring)]

    def shape(dims, dtype=BF16):
        return jax.ShapeDtypeStruct(dims, dtype)

    sources = [pltpu.with_memory_space_constraint(x, pltpu.HBM) for x in (keys, values, log_forget, write_rate, w_out)]
    total, inner, bases, writes, rows, w_half = call(
        states_kernel,
        (
            shape((heads, DK, 2 * DK)),
            shape((heads, 4, DK, 2 * DK)),
            shape((tokens, wide), F32),
            shape((tokens, wide), F32),
            shape((8, tokens), F32),
            shape((DK, w_out.shape[1])),
        ),
        [HBM] * 5,
        2_000_000_000,
        1_000_000,
        [
            pltpu.VMEM((tokens, wide), BF16),
            pltpu.VMEM((tokens, wide), BF16),
            pltpu.VMEM((heads, tokens), F32),
            pltpu.VMEM((heads, tokens), F32),
            pltpu.SemaphoreType.DMA((4,)),
            pltpu.SemaphoreType.DMA,
        ],
        (VMEM,) * 5 + (HBM,),
    )(*sources)

    core, lifted = call(
        reads_kernel,
        (shape((tokens, wide), F32), shape((tokens, wide))),
        [VMEM] * 7,
        1_000_000_000,
        1_000_000,
    )(queries, keys, bases, writes, rows, inner, level_weight)

    cores = [(i, i ^ 1) for i in range(seq)]
    theirs = lax.ppermute(total, "seq", cores)
    direct = lax.ppermute(w_half, "head", pairs)
    matrix = shape((heads, DK, DK))
    total, level, before = call(
        merge_kernel,
        (shape((heads, DK, 2 * DK)), matrix, matrix),
        [VMEM] * 2,
        40_000_000,
        500_000,
    )(total, theirs)
    collected = [level]

    def gathered(b):
        stride = 1 << b
        groups = [[i + k * stride for k in range(4)] for i in range(seq) if (i >> b) & 3 == 0]
        return lax.all_gather(total, "seq", axis=0, axis_index_groups=groups)

    for b in range(1, outer - 2, 2):
        total, low, high, before = call(
            lambda *refs, b=b: quad_kernel(b, *refs),
            (shape((heads, DK, 2 * DK)), matrix, matrix, matrix),
            [VMEM] * 2,
            100_000_000,
            1_000_000,
        )(gathered(b), before)
        collected += [low, high]
    four = gathered(outer - 2)
    keep, give = call(
        lambda *refs: finish_kernel(outer, ring // 2, *refs),
        (shape((tokens // 2, wide)), shape((tokens // 2, wide))),
        [VMEM] * (6 + outer - 2),
        100_000_000,
        1_000_000,
        [pltpu.VMEM((tokens, wide), BF16)],
    )(core, lifted, four, before, level_weight, gate, *collected)
    got = lax.ppermute(give, "head", pairs)
    columns = w_out.shape[1]
    step = columns // 4
    chunk = tokens // ring
    count = ring // 2
    lead = 2 * chunk
    rest = tokens // 2 - lead

    def by_columns(rows):
        return pl.BlockSpec((rows, step), lambda c: (0, c))

    whole = pl.BlockSpec((tokens // 2, wide), lambda c: (0, 0))

    def project(body, out_shape, in_specs, flops):
        return pl.pallas_call(
            body,
            grid=(columns // step,),
            out_shape=out_shape,
            in_specs=in_specs,
            out_specs=[by_columns(out.shape[0]) for out in out_shape],
            compiler_params=pltpu.CompilerParams(vmem_limit_bytes=16 << 20),
            cost_estimate=pl.CostEstimate(flops=flops, bytes_accessed=4_000_000, transcendentals=0),
        )

    (sums,) = project(
        project_own_kernel, [shape((tokens // 2, columns), F32)], [whole, by_columns(wide)], 300_000_000
    )(keep, w_out)
    got, direct, sums = lax.optimization_barrier((got, direct, sums))
    across = lax.ppermute(direct, "seq", cores)
    first, others = project(
        project_direct_kernel,
        [shape((lead, columns), F32), shape((rest, columns), F32)],
        [whole, by_columns(tokens // 2), by_columns(DK)],
        150_000_000,
    )(got, sums, direct)
    ends = project(
        lambda *refs: project_kernel(0, *refs),
        [shape((chunk, columns))] * 2,
        [whole, by_columns(lead), by_columns(DK)],
        40_000_000,
    )(got, first, across)
    middle = project(
        lambda *refs: project_kernel(lead, *refs),
        [shape((chunk, columns))] * (count - 2),
        [whole, by_columns(rest), by_columns(DK)],
        120_000_000,
    )(got, others, across) if count > 2 else []
    terms = [ends[0], *middle, ends[1]]
    return ring_sum(terms)


def solution(mesh):
    in_specs = (
        P("seq", "head"),
        P("seq", "head"),
        P("seq", "head"),
        P("seq", "head"),
        P("head", "seq"),
        P("head", "seq"),
        P("head", None, "seq"),
        P("head", None),
    )
    out_specs = P(("seq", "head"), None)
    return jax.shard_map(
        on_device, mesh=mesh, in_specs=in_specs, out_specs=out_specs, check_vma=False
    )
```

```python
import jax
import jax.numpy as jnp
from jax import lax
from jax.experimental import pallas as pl
from jax.experimental.pallas import tpu as pltpu
from jax.sharding import PartitionSpec as P

DK = 128
BLOCK = 64
TILE = 128
EPSILON = 1e-06
F32 = jnp.float32
BF16 = jnp.bfloat16
VMEM = pl.BlockSpec(memory_space=pltpu.VMEM)
HBM = pl.BlockSpec(memory_space=pltpu.HBM)


def dot(left, right, dims=((1,), (0,)), precision=None):
    return lax.dot_general(left, right, (dims, ((), ())), precision=precision, preferred_element_type=F32)


def halves(matrix):
    high = matrix.astype(BF16)
    return high, (matrix - high.astype(F32)).astype(BF16)


def paired(matrix):
    return jnp.concatenate(halves(matrix), axis=1)


def twice(matrix):
    return jnp.concatenate([matrix, matrix], axis=0)


def product(left, right):
    wide = dot(left, twice(right))
    return wide[:, :DK] + wide[:, DK:]


def tile_masks():
    row = lax.broadcasted_iota(jnp.int32, (TILE, TILE), 0)
    col = lax.broadcasted_iota(jnp.int32, (TILE, TILE), 1)
    return row, col, row // BLOCK == col // BLOCK


def states_kernel(
    k_in, v_in, lf_in, wr_in, full_ref, x_ref, y_ref, w_ref, u_ref, rows_ref, half_ref,
    k_ref, v_ref, lf_ref, wr_ref, in_sems, half_sem,
):
    copies = [
        pltpu.make_async_copy(source, target, in_sems.at[i])
        for i, (source, target) in enumerate(((k_in, k_ref), (lf_in, lf_ref), (wr_in, wr_ref), (v_in, v_ref)))
    ]
    for copy in copies:
        copy.start()
    count = half_ref.shape[0]
    first = pl.multiple_of(lax.rem(lax.axis_index("seq"), 2) * count, count)
    half = pltpu.make_async_copy(full_ref.at[pl.ds(first, count)], half_ref, half_sem)
    half.start()
    for copy in copies:
        copy.wait()
    tokens = k_ref.shape[0]
    heads = lf_ref.shape[0]
    tiles = tokens // TILE
    row, col, same = tile_masks()
    inclusive = same & (row >= col)
    strict = same & (row > col)
    eye = (row == col).astype(F32)

    def by_tile(ref):
        return jnp.concatenate([ref[:, t * TILE : (t + 1) * TILE] for t in range(tiles)], axis=0)

    log_forget, rate = by_tile(lf_ref), by_tile(wr_ref)
    exact = lax.Precision.HIGHEST
    cum = dot(log_forget, inclusive.astype(F32), ((1,), (1,)), exact)
    total = dot(log_forget, same.astype(F32), ((1,), (1,)), exact)
    count = tiles * heads
    pad = jnp.zeros((16 - 3 * count, TILE), F32)
    columns = jnp.concatenate([cum, total, rate, pad], axis=0).T
    units = [(t, h) for t in range(tiles) for h in range(heads)]
    lowers, keys, norms, inverses = [], [], [], []
    for n, (t, h) in enumerate(units):
        key = k_ref[t * TILE : (t + 1) * TILE, h * DK : (h + 1) * DK]
        key_f = key.astype(F32)
        key_key = dot(key, key, ((1,), (1,)))
        inv_col = lax.rsqrt(jnp.sum(key_f * key_f, axis=1, keepdims=True) + EPSILON)
        inv_row = lax.rsqrt(jnp.sum(key_key * eye, axis=0, keepdims=True) + EPSILON)
        rate_col = columns[:, 2 * count + n : 2 * count + n + 1]
        lower = jnp.where(strict, key_key * (rate_col * inv_col) * inv_row, 0.0)
        inverses.append(eye - jnp.where(row // 2 == col // 2, lower, 0.0))
        lowers.append(paired(lower))
        keys.append((key, key_f))
        norms.append((inv_col, inv_row))
    width = 2
    while width < BLOCK:
        band = ((row // width != col // width) & (row // (2 * width) == col // (2 * width))).astype(F32).astype(BF16)
        band = jnp.concatenate([band, band], axis=1)
        split = [paired(inverse) for inverse in inverses]
        inner = [product(lowers[n] * band, split[n]) for n in range(count)]
        inverses = [inverses[n] - product(split[n], paired(inner[n])) for n in range(count)]
        width *= 2
    blocks = tokens // BLOCK
    leaf = {}
    for n, (t, h) in enumerate(units):
        rows = slice(t * TILE, (t + 1) * TILE)
        lanes = slice(h * DK, (h + 1) * DK)
        key, key_f = keys[n]
        inv_col, inv_row = norms[n]
        cum_col = columns[:, n : n + 1]
        total_col = columns[:, count + n : count + n + 1]
        fading = jnp.exp(jnp.where(inclusive, cum_col - cum[n : n + 1], -1e30))
        solved = inverses[n] * rate[n : n + 1]
        bases = dot(paired(solved * inv_row), twice(key))
        writes = dot(paired(solved * fading), twice(v_ref[rows, lanes]))
        w_ref[rows, lanes] = bases
        u_ref[rows, lanes] = writes
        both = jnp.concatenate([writes * (jnp.exp(total_col - cum_col) * inv_col), bases * inv_col], axis=1)
        turned = key_f.T
        picked = [jnp.where(col // BLOCK == b, turned, 0.0).astype(BF16) for b in range(TILE // BLOCK)]
        picked = jnp.concatenate([jnp.concatenate([p, p], axis=1) for p in picked], axis=0)
        raw = dot(picked, jnp.concatenate(halves(both), axis=0))
        for b in range(TILE // BLOCK):
            part = raw[b * DK : (b + 1) * DK]
            fade = jnp.exp(total[n : n + 1, b * BLOCK : b * BLOCK + 1])
            leaf[h, t * (TILE // BLOCK) + b] = part[:, :DK], fade * (eye - part[:, DK:])

    def merge(lead, trail):
        moved = dot(trail[1].astype(BF16), jnp.concatenate(lead, axis=1).astype(BF16))
        return moved[:, :DK] + trail[0], moved[:, DK:]

    def stored(state):
        return jnp.concatenate(state, axis=1).astype(BF16)

    firsts = [merge(leaf[h, 0], leaf[h, 1]) for h in range(heads)]
    seconds = [merge(leaf[h, 2], leaf[h, 3]) for h in range(heads)]
    for h in range(heads):
        x_ref[h] = stored(merge(firsts[h], seconds[h]))
    for h in range(heads):
        y_ref[h, 0] = stored(leaf[h, 0])
        y_ref[h, 1] = stored(firsts[h])
        y_ref[h, 2] = dot(leaf[h, 2][1].astype(BF16), stored(firsts[h])).astype(BF16)
        y_ref[h, 3] = stored(leaf[h, 2])
    filler = jnp.zeros((8 - 2 * heads, TILE), F32)
    for t in range(tiles):
        found = [norms[t * heads + h][1] for h in range(heads)]
        rows_ref[:, t * TILE : (t + 1) * TILE] = jnp.concatenate(
            [cum[t * heads : (t + 1) * heads]] + found + [filler], axis=0
        )
    half.wait()


def reads_kernel(q_ref, k_ref, w_ref, u_ref, rows_ref, y_ref, lw_ref, core_ref, lift_ref):
    tokens = k_ref.shape[0]
    heads = y_ref.shape[0]
    row, col, same = tile_masks()
    inclusive = same & (row >= col)
    rows = rows_ref[...]
    columns = rows.T
    levels = lw_ref.shape[1]
    weights = lw_ref[...].reshape(heads * levels, tokens).T
    for h in range(heads):
        lanes = slice(h * DK, (h + 1) * DK)

        def weight(level, span):
            at = h * levels + level
            return weights[span, at : at + 1]

        owns, reaches = [], []
        for t in range(tokens // TILE):
            here = slice(t * TILE, (t + 1) * TILE)
            query = q_ref[here, lanes]
            query_f = query.astype(F32)
            inv_query = lax.rsqrt(jnp.sum(query_f * query_f, axis=1, keepdims=True) + EPSILON)
            query_key = dot(query, k_ref[here, lanes], ((1,), (1,))) * inv_query * rows[heads + h : heads + h + 1, here]
            cum_col = columns[here, h : h + 1]
            fading = jnp.exp(jnp.where(inclusive, cum_col - rows[h : h + 1, here], -1e30))
            owns.append(product(paired(query_key * fading), paired(u_ref[here, lanes])))
            masked = jnp.where(inclusive, query_key, 0.0)
            reach = query_f * inv_query - product(paired(masked), paired(w_ref[here, lanes]))
            reaches.append((jnp.exp(cum_col) * reach).astype(BF16))
        spans = [slice(g * BLOCK, (g + 1) * BLOCK) for g in range(4)]
        own = [owns[g // 2][spans[g % 2]] for g in range(4)]
        reach = [reaches[g // 2][spans[g % 2]] for g in range(4)]
        read1 = dot(reach[1], y_ref[h, 0])
        read2 = dot(reach[2], y_ref[h, 1])
        read3 = dot(reach[3], y_ref[h, 2])
        near3 = dot(reach[3], y_ref[h, 3, :, :DK])
        core_ref[spans[0], lanes] = weight(0, spans[0]) * own[0]
        core_ref[spans[1], lanes] = weight(0, spans[1]) * own[1] + weight(1, spans[1]) * read1[:, :DK]
        core_ref[spans[2], lanes] = weight(0, spans[2]) * own[2] + weight(2, spans[2]) * read2[:, :DK]
        core_ref[spans[3], lanes] = (
            weight(0, spans[3]) * own[3] + weight(1, spans[3]) * near3 + weight(2, spans[3]) * read3[:, :DK]
        )
        lift_ref[spans[0], lanes] = reach[0]
        lift_ref[spans[1], lanes] = read1[:, DK:].astype(BF16)
        lift_ref[spans[2], lanes] = read2[:, DK:].astype(BF16)
        lift_ref[spans[3], lanes] = read3[:, DK:].astype(BF16)


def merge_kernel(mine_ref, theirs_ref, total_ref, level_ref, after_ref):
    upper = lax.rem(lax.axis_index("seq"), 2) == 1
    same = lax.broadcasted_iota(jnp.int32, (DK, DK), 0) == lax.broadcasted_iota(jnp.int32, (DK, DK), 1)
    for h in range(mine_ref.shape[0]):
        mine, theirs = mine_ref[h], theirs_ref[h]
        total_ref[h] = joined(jnp.where(upper, theirs, mine), jnp.where(upper, mine, theirs))
        level_ref[h] = jnp.where(upper, theirs[:, :DK], jnp.zeros((DK, DK), BF16))
        after_ref[h] = jnp.where(upper, theirs[:, DK:], same.astype(BF16))


def joined(lead, trail):
    moved = dot(trail[:, DK:], lead)
    return jnp.concatenate([moved[:, :DK] + trail[:, :DK].astype(F32), moved[:, DK:]], axis=1).astype(BF16)


def two_levels(digit, four_ref, before_ref, h):
    before = before_ref[h]
    near = dot(before, four_ref[jnp.maximum(digit - 1, 0), h]).astype(BF16)
    odd = lax.rem(digit, 2) == 1
    low = jnp.where(odd, near[:, :DK], jnp.zeros((DK, DK), BF16))
    before = jnp.where(odd, near[:, DK:], before)
    first = joined(four_ref[0, h], four_ref[1, h])
    far = dot(before, first).astype(BF16)
    upper = digit >= 2
    high = jnp.where(upper, far[:, :DK], jnp.zeros((DK, DK), BF16))
    return low, high, jnp.where(upper, far[:, DK:], before), first


def quad_kernel(bit, four_ref, before_ref, total_ref, low_ref, high_ref, after_ref):
    digit = (lax.axis_index("seq") >> bit) & 3
    for h in range(before_ref.shape[0]):
        low_ref[h], high_ref[h], after_ref[h], first = two_levels(digit, four_ref, before_ref, h)
        total_ref[h] = joined(first, joined(four_ref[2, h], four_ref[3, h]))


def hop_order(ring):
    return [0, ring - 1] + list(range(1, ring - 1))


def finish_kernel(outer, ring, core_ref, lift_ref, four_ref, before_ref, lw_ref, gate_ref, *rest):
    level_refs, keep_ref, give_ref, norm_ref = rest[:-3], rest[-3], rest[-2], rest[-1]
    digit = (lax.axis_index("seq") >> (outer - 2)) & 3
    heads = before_ref.shape[0]
    tokens = core_ref.shape[0]
    levels = lw_ref.shape[1]
    weights = lw_ref[...].reshape(heads * levels, tokens).T
    for h in range(heads):
        lanes = slice(h * DK, (h + 1) * DK)
        lifted = lift_ref[:, lanes].astype(F32)
        low, high, _, _ = two_levels(digit, four_ref, before_ref, h)
        stack = [level_ref[h] for level_ref in level_refs] + [low, high]
        scaled = []
        for b in range(outer):
            at = h * levels + levels - outer + b
            scaled.append((lifted * weights[:, at : at + 1]).astype(BF16))
        core = core_ref[:, lanes] + dot(jnp.concatenate(scaled, axis=1), jnp.concatenate(stack, axis=0))
        core = core * lax.rsqrt(jnp.mean(core * core, axis=1, keepdims=True) + EPSILON)
        gate = gate_ref[:, lanes].astype(F32)
        norm_ref[:, lanes] = (core * (gate / (1.0 + jnp.exp(-gate)))).astype(BF16)
    chunk = tokens // (2 * ring)
    pair = lax.axis_index("head") // 2
    parity = lax.rem(lax.axis_index("head"), 2)
    side = 1 - 2 * lax.rem(lax.axis_index("head") + lax.axis_index("seq"), 2)
    for n, j in enumerate(hop_order(ring)):
        kept = 2 * lax.rem(pair + ring + side * (ring // 2 - j), ring) + parity
        given = 2 * lax.rem(pair + ring - side * (ring // 2 - j), ring) + 1 - parity
        rows = slice(n * chunk, (n + 1) * chunk)
        keep_ref[rows] = norm_ref[pl.ds(pl.multiple_of(kept * chunk, chunk), chunk)]
        give_ref[rows] = norm_ref[pl.ds(pl.multiple_of(given * chunk, chunk), chunk)]


def project_own_kernel(keep_ref, mine_ref, first_ref, others_ref):
    sums = dot(keep_ref[...], mine_ref[...])
    count = first_ref.shape[0]
    first_ref[...] = sums[:count]
    others_ref[...] = sums[count:]


def project_kernel(start, got_ref, sums_ref, direct_ref, across_ref, *out_refs):
    second = lax.rem(lax.axis_index("seq"), 2) == 1
    rows = slice(start, start + sums_ref.shape[0])
    one, two = got_ref[rows, :DK], got_ref[rows, DK:]
    sums = (
        sums_ref[...]
        + dot(jnp.where(second, two, one), direct_ref[...])
        + dot(jnp.where(second, one, two), across_ref[...])
    )
    chunk = out_refs[0].shape[0]
    for j, out_ref in enumerate(out_refs):
        out_ref[...] = sums[j * chunk : (j + 1) * chunk].astype(BF16)


def call(body, out_shape, specs, flops, bytes_accessed, scratch=(), out_specs=None, mib=16):
    return pl.pallas_call(
        body,
        out_shape=out_shape,
        in_specs=specs,
        out_specs=jax.tree.map(lambda _: VMEM, out_shape) if out_specs is None else out_specs,
        scratch_shapes=scratch,
        compiler_params=pltpu.CompilerParams(vmem_limit_bytes=mib << 20),
        cost_estimate=pl.CostEstimate(flops=flops, bytes_accessed=bytes_accessed, transcendentals=0),
    )


def ring_sum(terms):
    ring = len(terms)
    half = ring // 2
    count = 2 * ring
    slabs = lax.axis_size("seq")

    def hop(block, way):
        route = []
        for s in range(slabs):
            for z in range(count):
                step = 2 * way * (1 - 2 * ((s + z) % 2))
                route.append((s * count + z, s * count + (z + step) % count))
        return lax.ppermute(block, ("seq", "head"), route).astype(F32)

    ahead, behind = terms[0], terms[ring - 1]
    for t in range(1, half):
        ahead = (hop(ahead, 1) + terms[t].astype(F32)).astype(BF16)
        if t < half - 1:
            behind = (hop(behind, -1) + terms[ring - 1 - t].astype(F32)).astype(BF16)
    ahead = hop(ahead, 1) + terms[half].astype(F32)
    return (ahead + hop(behind, -1) if half > 1 else ahead).astype(BF16)


def on_device(queries, keys, values, gate, log_forget, write_rate, level_weight, w_out):
    tokens = queries.shape[0]
    heads = log_forget.shape[0]
    seq = lax.axis_size("seq")
    outer = seq.bit_length() - 1
    ring = lax.axis_size("head")
    wide = heads * DK
    pairs = [(i, i ^ 1) for i in range(ring)]

    def shape(dims, dtype=BF16):
        return jax.ShapeDtypeStruct(dims, dtype)

    sources = [pltpu.with_memory_space_constraint(x, pltpu.HBM) for x in (keys, values, log_forget, write_rate, w_out)]
    total, inner, bases, writes, rows, w_half = call(
        states_kernel,
        (
            shape((heads, DK, 2 * DK)),
            shape((heads, 4, DK, 2 * DK)),
            shape((tokens, wide), F32),
            shape((tokens, wide), F32),
            shape((8, tokens), F32),
            shape((DK, w_out.shape[1])),
        ),
        [HBM] * 5,
        2_000_000_000,
        1_000_000,
        [
            pltpu.VMEM((tokens, wide), BF16),
            pltpu.VMEM((tokens, wide), BF16),
            pltpu.VMEM((heads, tokens), F32),
            pltpu.VMEM((heads, tokens), F32),
            pltpu.SemaphoreType.DMA((4,)),
            pltpu.SemaphoreType.DMA,
        ],
        (VMEM,) * 5 + (HBM,),
    )(*sources)

    core, lifted = call(
        reads_kernel,
        (shape((tokens, wide), F32), shape((tokens, wide))),
        [VMEM] * 7,
        1_000_000_000,
        1_000_000,
    )(queries, keys, bases, writes, rows, inner, level_weight)

    cores = [(i, i ^ 1) for i in range(seq)]
    theirs = lax.ppermute(total, "seq", cores)
    direct = lax.ppermute(w_half, "head", pairs)
    matrix = shape((heads, DK, DK))
    total, level, before = call(
        merge_kernel,
        (shape((heads, DK, 2 * DK)), matrix, matrix),
        [VMEM] * 2,
        40_000_000,
        500_000,
    )(total, theirs)
    collected = [level]

    def gathered(b):
        stride = 1 << b
        groups = [[i + k * stride for k in range(4)] for i in range(seq) if (i >> b) & 3 == 0]
        return lax.all_gather(total, "seq", axis=0, axis_index_groups=groups)

    for b in range(1, outer - 2, 2):
        total, low, high, before = call(
            lambda *refs, b=b: quad_kernel(b, *refs),
            (shape((heads, DK, 2 * DK)), matrix, matrix, matrix),
            [VMEM] * 2,
            100_000_000,
            1_000_000,
        )(gathered(b), before)
        collected += [low, high]
    four = gathered(outer - 2)
    keep, give = call(
        lambda *refs: finish_kernel(outer, ring // 2, *refs),
        (shape((tokens // 2, wide)), shape((tokens // 2, wide))),
        [VMEM] * (6 + outer - 2),
        100_000_000,
        1_000_000,
        [pltpu.VMEM((tokens, wide), BF16)],
    )(core, lifted, four, before, level_weight, gate, *collected)
    give, direct = lax.optimization_barrier((give, direct))
    got = lax.ppermute(give, "head", pairs)
    across = lax.ppermute(direct, "seq", cores)
    columns = w_out.shape[1]
    step = columns // 4
    chunk = tokens // ring
    count = ring // 2
    lead = 2 * chunk
    rest = tokens // 2 - lead

    def by_columns(rows):
        return pl.BlockSpec((rows, step), lambda c: (0, c))

    whole = pl.BlockSpec((tokens // 2, wide), lambda c: (0, 0))

    def project(body, out_shape, in_specs, flops):
        return pl.pallas_call(
            body,
            grid=(columns // step,),
            out_shape=out_shape,
            in_specs=in_specs,
            out_specs=[by_columns(out.shape[0]) for out in out_shape],
            compiler_params=pltpu.CompilerParams(vmem_limit_bytes=16 << 20),
            cost_estimate=pl.CostEstimate(flops=flops, bytes_accessed=4_000_000, transcendentals=0),
        )

    first, others = project(
        project_own_kernel,
        [shape((lead, columns), F32), shape((rest, columns), F32)],
        [whole, by_columns(wide)],
        300_000_000,
    )(keep, w_out)
    ends = project(
        lambda *refs: project_kernel(0, *refs),
        [shape((chunk, columns))] * 2,
        [whole, by_columns(lead), by_columns(DK), by_columns(DK)],
        80_000_000,
    )(got, first, direct, across)
    middle = project(
        lambda *refs: project_kernel(lead, *refs),
        [shape((chunk, columns))] * (count - 2),
        [whole, by_columns(rest), by_columns(DK), by_columns(DK)],
        240_000_000,
    )(got, others, direct, across) if count > 2 else []
    terms = [ends[0], *middle, ends[1]]
    return ring_sum(terms)


def solution(mesh):
    in_specs = (
        P("seq", "head"),
        P("seq", "head"),
        P("seq", "head"),
        P("seq", "head"),
        P("head", "seq"),
        P("head", "seq"),
        P("head", None, "seq"),
        P("head", None),
    )
    out_specs = P(("seq", "head"), None)
    return jax.shard_map(
        on_device, mesh=mesh, in_specs=in_specs, out_specs=out_specs, check_vma=False
    )
```

```python
import jax
import jax.numpy as jnp
from jax import lax
from jax.experimental import pallas as pl
from jax.experimental.pallas import tpu as pltpu
from jax.sharding import PartitionSpec as P

DK = 128
BLOCK = 64
TILE = 128
EPSILON = 1e-06
F32 = jnp.float32
BF16 = jnp.bfloat16
VMEM = pl.BlockSpec(memory_space=pltpu.VMEM)
HBM = pl.BlockSpec(memory_space=pltpu.HBM)


def dot(left, right, dims=((1,), (0,)), precision=None):
    return lax.dot_general(left, right, (dims, ((), ())), precision=precision, preferred_element_type=F32)


def halves(matrix):
    high = matrix.astype(BF16)
    return high, (matrix - high.astype(F32)).astype(BF16)


def paired(matrix):
    return jnp.concatenate(halves(matrix), axis=1)


def twice(matrix):
    return jnp.concatenate([matrix, matrix], axis=0)


def product(left, right):
    wide = dot(left, twice(right))
    return wide[:, :DK] + wide[:, DK:]


def tile_masks():
    row = lax.broadcasted_iota(jnp.int32, (TILE, TILE), 0)
    col = lax.broadcasted_iota(jnp.int32, (TILE, TILE), 1)
    return row, col, row // BLOCK == col // BLOCK


def states_kernel(
    k_in, v_in, lf_in, wr_in, full_ref, x_ref, y_ref, w_ref, u_ref, rows_ref, half_ref,
    k_ref, v_ref, lf_ref, wr_ref, in_sems, half_sem,
):
    copies = [
        pltpu.make_async_copy(source, target, in_sems.at[i])
        for i, (source, target) in enumerate(((k_in, k_ref), (lf_in, lf_ref), (wr_in, wr_ref), (v_in, v_ref)))
    ]
    for copy in copies:
        copy.start()
    count = half_ref.shape[0]
    first = pl.multiple_of(lax.rem(lax.axis_index("seq"), 2) * count, count)
    half = pltpu.make_async_copy(full_ref.at[pl.ds(first, count)], half_ref, half_sem)
    half.start()
    for copy in copies:
        copy.wait()
    tokens = k_ref.shape[0]
    heads = lf_ref.shape[0]
    tiles = tokens // TILE
    row, col, same = tile_masks()
    inclusive = same & (row >= col)
    strict = same & (row > col)
    eye = (row == col).astype(F32)

    def by_tile(ref):
        return jnp.concatenate([ref[:, t * TILE : (t + 1) * TILE] for t in range(tiles)], axis=0)

    log_forget, rate = by_tile(lf_ref), by_tile(wr_ref)
    exact = lax.Precision.HIGHEST
    cum = dot(log_forget, inclusive.astype(F32), ((1,), (1,)), exact)
    total = dot(log_forget, same.astype(F32), ((1,), (1,)), exact)
    count = tiles * heads
    pad = jnp.zeros((16 - 3 * count, TILE), F32)
    columns = jnp.concatenate([cum, total, rate, pad], axis=0).T
    units = [(t, h) for t in range(tiles) for h in range(heads)]
    lowers, keys, norms, inverses = [], [], [], []
    for n, (t, h) in enumerate(units):
        key = k_ref[t * TILE : (t + 1) * TILE, h * DK : (h + 1) * DK]
        key_f = key.astype(F32)
        key_key = dot(key, key, ((1,), (1,)))
        inv_col = lax.rsqrt(jnp.sum(key_f * key_f, axis=1, keepdims=True) + EPSILON)
        inv_row = lax.rsqrt(jnp.sum(key_key * eye, axis=0, keepdims=True) + EPSILON)
        rate_col = columns[:, 2 * count + n : 2 * count + n + 1]
        lower = jnp.where(strict, key_key * (rate_col * inv_col) * inv_row, 0.0)
        inverses.append(eye - jnp.where(row // 2 == col // 2, lower, 0.0))
        lowers.append(paired(lower))
        keys.append((key, key_f))
        norms.append((inv_col, inv_row))
    width = 2
    while width < BLOCK:
        band = ((row // width != col // width) & (row // (2 * width) == col // (2 * width))).astype(F32).astype(BF16)
        band = jnp.concatenate([band, band], axis=1)
        split = [paired(inverse) for inverse in inverses]
        inner = [product(lowers[n] * band, split[n]) for n in range(count)]
        inverses = [inverses[n] - product(split[n], paired(inner[n])) for n in range(count)]
        width *= 2
    blocks = tokens // BLOCK
    leaf = {}
    for n, (t, h) in enumerate(units):
        rows = slice(t * TILE, (t + 1) * TILE)
        lanes = slice(h * DK, (h + 1) * DK)
        key, key_f = keys[n]
        inv_col, inv_row = norms[n]
        cum_col = columns[:, n : n + 1]
        total_col = columns[:, count + n : count + n + 1]
        fading = jnp.exp(jnp.where(inclusive, cum_col - cum[n : n + 1], -1e30))
        solved = inverses[n] * rate[n : n + 1]
        bases = dot(paired(solved * inv_row), twice(key))
        writes = dot(paired(solved * fading), twice(v_ref[rows, lanes]))
        w_ref[rows, lanes] = bases
        u_ref[rows, lanes] = writes
        both = jnp.concatenate([writes * (jnp.exp(total_col - cum_col) * inv_col), bases * inv_col], axis=1)
        turned = key_f.T
        picked = [jnp.where(col // BLOCK == b, turned, 0.0).astype(BF16) for b in range(TILE // BLOCK)]
        picked = jnp.concatenate([jnp.concatenate([p, p], axis=1) for p in picked], axis=0)
        raw = dot(picked, jnp.concatenate(halves(both), axis=0))
        for b in range(TILE // BLOCK):
            part = raw[b * DK : (b + 1) * DK]
            fade = jnp.exp(total[n : n + 1, b * BLOCK : b * BLOCK + 1])
            leaf[h, t * (TILE // BLOCK) + b] = part[:, :DK], fade * (eye - part[:, DK:])

    def merge(lead, trail):
        moved = dot(trail[1].astype(BF16), jnp.concatenate(lead, axis=1).astype(BF16))
        return moved[:, :DK] + trail[0], moved[:, DK:]

    def stored(state):
        return jnp.concatenate(state, axis=1).astype(BF16)

    firsts = [merge(leaf[h, 0], leaf[h, 1]) for h in range(heads)]
    seconds = [merge(leaf[h, 2], leaf[h, 3]) for h in range(heads)]
    for h in range(heads):
        x_ref[h] = stored(merge(firsts[h], seconds[h]))
    for h in range(heads):
        y_ref[h, 0] = stored(leaf[h, 0])
        y_ref[h, 1] = stored(firsts[h])
        y_ref[h, 2] = dot(leaf[h, 2][1].astype(BF16), stored(firsts[h])).astype(BF16)
        y_ref[h, 3] = stored(leaf[h, 2])
    filler = jnp.zeros((8 - 2 * heads, TILE), F32)
    for t in range(tiles):
        found = [norms[t * heads + h][1] for h in range(heads)]
        rows_ref[:, t * TILE : (t + 1) * TILE] = jnp.concatenate(
            [cum[t * heads : (t + 1) * heads]] + found + [filler], axis=0
        )
    half.wait()


def reads_kernel(q_ref, k_ref, w_ref, u_ref, rows_ref, y_ref, lw_ref, core_ref, lift_ref):
    tokens = k_ref.shape[0]
    heads = y_ref.shape[0]
    row, col, same = tile_masks()
    inclusive = same & (row >= col)
    rows = rows_ref[...]
    columns = rows.T
    levels = lw_ref.shape[1]
    weights = lw_ref[...].reshape(heads * levels, tokens).T
    for h in range(heads):
        lanes = slice(h * DK, (h + 1) * DK)

        def weight(level, span):
            at = h * levels + level
            return weights[span, at : at + 1]

        owns, reaches = [], []
        for t in range(tokens // TILE):
            here = slice(t * TILE, (t + 1) * TILE)
            query = q_ref[here, lanes]
            query_f = query.astype(F32)
            inv_query = lax.rsqrt(jnp.sum(query_f * query_f, axis=1, keepdims=True) + EPSILON)
            query_key = dot(query, k_ref[here, lanes], ((1,), (1,))) * inv_query * rows[heads + h : heads + h + 1, here]
            cum_col = columns[here, h : h + 1]
            fading = jnp.exp(jnp.where(inclusive, cum_col - rows[h : h + 1, here], -1e30))
            owns.append(product(paired(query_key * fading), paired(u_ref[here, lanes])))
            masked = jnp.where(inclusive, query_key, 0.0)
            reach = query_f * inv_query - product(paired(masked), paired(w_ref[here, lanes]))
            reaches.append((jnp.exp(cum_col) * reach).astype(BF16))
        spans = [slice(g * BLOCK, (g + 1) * BLOCK) for g in range(4)]
        own = [owns[g // 2][spans[g % 2]] for g in range(4)]
        reach = [reaches[g // 2][spans[g % 2]] for g in range(4)]
        read1 = dot(reach[1], y_ref[h, 0])
        read2 = dot(reach[2], y_ref[h, 1])
        read3 = dot(reach[3], y_ref[h, 2])
        near3 = dot(reach[3], y_ref[h, 3, :, :DK])
        core_ref[spans[0], lanes] = weight(0, spans[0]) * own[0]
        core_ref[spans[1], lanes] = weight(0, spans[1]) * own[1] + weight(1, spans[1]) * read1[:, :DK]
        core_ref[spans[2], lanes] = weight(0, spans[2]) * own[2] + weight(2, spans[2]) * read2[:, :DK]
        core_ref[spans[3], lanes] = (
            weight(0, spans[3]) * own[3] + weight(1, spans[3]) * near3 + weight(2, spans[3]) * read3[:, :DK]
        )
        lift_ref[spans[0], lanes] = reach[0]
        lift_ref[spans[1], lanes] = read1[:, DK:].astype(BF16)
        lift_ref[spans[2], lanes] = read2[:, DK:].astype(BF16)
        lift_ref[spans[3], lanes] = read3[:, DK:].astype(BF16)


def merge_kernel(mine_ref, theirs_ref, total_ref, level_ref, after_ref):
    upper = lax.rem(lax.axis_index("seq"), 2) == 1
    same = lax.broadcasted_iota(jnp.int32, (DK, DK), 0) == lax.broadcasted_iota(jnp.int32, (DK, DK), 1)
    for h in range(mine_ref.shape[0]):
        mine, theirs = mine_ref[h], theirs_ref[h]
        total_ref[h] = joined(jnp.where(upper, theirs, mine), jnp.where(upper, mine, theirs))
        level_ref[h] = jnp.where(upper, theirs[:, :DK], jnp.zeros((DK, DK), BF16))
        after_ref[h] = jnp.where(upper, theirs[:, DK:], same.astype(BF16))


def joined(lead, trail):
    moved = dot(trail[:, DK:], lead)
    return jnp.concatenate([moved[:, :DK] + trail[:, :DK].astype(F32), moved[:, DK:]], axis=1).astype(BF16)


def two_levels(digit, four_ref, before_ref, h):
    before = before_ref[h]
    near = dot(before, four_ref[jnp.maximum(digit - 1, 0), h]).astype(BF16)
    odd = lax.rem(digit, 2) == 1
    low = jnp.where(odd, near[:, :DK], jnp.zeros((DK, DK), BF16))
    before = jnp.where(odd, near[:, DK:], before)
    first = joined(four_ref[0, h], four_ref[1, h])
    far = dot(before, first).astype(BF16)
    upper = digit >= 2
    high = jnp.where(upper, far[:, :DK], jnp.zeros((DK, DK), BF16))
    return low, high, jnp.where(upper, far[:, DK:], before), first


def quad_kernel(bit, four_ref, before_ref, total_ref, low_ref, high_ref, after_ref):
    digit = (lax.axis_index("seq") >> bit) & 3
    for h in range(before_ref.shape[0]):
        low_ref[h], high_ref[h], after_ref[h], first = two_levels(digit, four_ref, before_ref, h)
        total_ref[h] = joined(first, joined(four_ref[2, h], four_ref[3, h]))


def hop_order(ring):
    return [0, ring - 1] + list(range(1, ring - 1))


def finish_kernel(outer, ring, core_ref, lift_ref, four_ref, before_ref, lw_ref, gate_ref, *rest):
    level_refs, keep_ref, give_ref, norm_ref = rest[:-3], rest[-3], rest[-2], rest[-1]
    digit = (lax.axis_index("seq") >> (outer - 2)) & 3
    heads = before_ref.shape[0]
    tokens = core_ref.shape[0]
    levels = lw_ref.shape[1]
    weights = lw_ref[...].reshape(heads * levels, tokens).T
    for h in range(heads):
        lanes = slice(h * DK, (h + 1) * DK)
        lifted = lift_ref[:, lanes].astype(F32)
        low, high, _, _ = two_levels(digit, four_ref, before_ref, h)
        stack = [level_ref[h] for level_ref in level_refs] + [low, high]
        scaled = []
        for b in range(outer):
            at = h * levels + levels - outer + b
            scaled.append((lifted * weights[:, at : at + 1]).astype(BF16))
        core = core_ref[:, lanes] + dot(jnp.concatenate(scaled, axis=1), jnp.concatenate(stack, axis=0))
        core = core * lax.rsqrt(jnp.mean(core * core, axis=1, keepdims=True) + EPSILON)
        gate = gate_ref[:, lanes].astype(F32)
        norm_ref[:, lanes] = (core * (gate / (1.0 + jnp.exp(-gate)))).astype(BF16)
    chunk = tokens // (2 * ring)
    pair = lax.axis_index("head") // 2
    parity = lax.rem(lax.axis_index("head"), 2)
    side = 1 - 2 * parity
    for n, j in enumerate(hop_order(ring)):
        kept = 2 * lax.rem(pair + ring + side * (ring // 2 - j), ring) + parity
        given = 2 * lax.rem(pair + ring - side * (ring // 2 - j), ring) + 1 - parity
        rows = slice(n * chunk, (n + 1) * chunk)
        keep_ref[rows] = norm_ref[pl.ds(pl.multiple_of(kept * chunk, chunk), chunk)]
        give_ref[rows] = norm_ref[pl.ds(pl.multiple_of(given * chunk, chunk), chunk)]


def project_own_kernel(keep_ref, mine_ref, first_ref, others_ref):
    sums = dot(keep_ref[...], mine_ref[...])
    count = first_ref.shape[0]
    first_ref[...] = sums[:count]
    others_ref[...] = sums[count:]


def project_kernel(start, got_ref, sums_ref, direct_ref, across_ref, *out_refs):
    second = lax.rem(lax.axis_index("seq"), 2) == 1
    rows = slice(start, start + sums_ref.shape[0])
    one, two = got_ref[rows, :DK], got_ref[rows, DK:]
    sums = (
        sums_ref[...]
        + dot(jnp.where(second, two, one), direct_ref[...])
        + dot(jnp.where(second, one, two), across_ref[...])
    )
    chunk = out_refs[0].shape[0]
    for j, out_ref in enumerate(out_refs):
        out_ref[...] = sums[j * chunk : (j + 1) * chunk].astype(BF16)


def call(body, out_shape, specs, flops, bytes_accessed, scratch=(), out_specs=None, mib=16):
    return pl.pallas_call(
        body,
        out_shape=out_shape,
        in_specs=specs,
        out_specs=jax.tree.map(lambda _: VMEM, out_shape) if out_specs is None else out_specs,
        scratch_shapes=scratch,
        compiler_params=pltpu.CompilerParams(vmem_limit_bytes=mib << 20),
        cost_estimate=pl.CostEstimate(flops=flops, bytes_accessed=bytes_accessed, transcendentals=0),
    )


def ring_sum(terms):
    ring = len(terms)
    half = ring // 2
    count = 2 * ring

    def hop(block, way):
        route = [(z, (z + 2 * way * (1 - 2 * (z % 2))) % count) for z in range(count)]
        return lax.ppermute(block, "head", route).astype(F32)

    ahead, behind = terms[0], terms[ring - 1]
    for t in range(1, half):
        ahead = (hop(ahead, 1) + terms[t].astype(F32)).astype(BF16)
        if t < half - 1:
            behind = (hop(behind, -1) + terms[ring - 1 - t].astype(F32)).astype(BF16)
    ahead = hop(ahead, 1) + terms[half].astype(F32)
    return (ahead + hop(behind, -1) if half > 1 else ahead).astype(BF16)


def on_device(queries, keys, values, gate, log_forget, write_rate, level_weight, w_out):
    tokens = queries.shape[0]
    heads = log_forget.shape[0]
    seq = lax.axis_size("seq")
    outer = seq.bit_length() - 1
    ring = lax.axis_size("head")
    wide = heads * DK
    pairs = [(i, i ^ 1) for i in range(ring)]

    def shape(dims, dtype=BF16):
        return jax.ShapeDtypeStruct(dims, dtype)

    sources = [pltpu.with_memory_space_constraint(x, pltpu.HBM) for x in (keys, values, log_forget, write_rate, w_out)]
    total, inner, bases, writes, rows, w_half = call(
        states_kernel,
        (
            shape((heads, DK, 2 * DK)),
            shape((heads, 4, DK, 2 * DK)),
            shape((tokens, wide), F32),
            shape((tokens, wide), F32),
            shape((8, tokens), F32),
            shape((DK, w_out.shape[1])),
        ),
        [HBM] * 5,
        2_000_000_000,
        1_000_000,
        [
            pltpu.VMEM((tokens, wide), BF16),
            pltpu.VMEM((tokens, wide), BF16),
            pltpu.VMEM((heads, tokens), F32),
            pltpu.VMEM((heads, tokens), F32),
            pltpu.SemaphoreType.DMA((4,)),
            pltpu.SemaphoreType.DMA,
        ],
        (VMEM,) * 5 + (HBM,),
    )(*sources)

    core, lifted = call(
        reads_kernel,
        (shape((tokens, wide), F32), shape((tokens, wide))),
        [VMEM] * 7,
        1_000_000_000,
        1_000_000,
    )(queries, keys, bases, writes, rows, inner, level_weight)

    cores = [(i, i ^ 1) for i in range(seq)]
    theirs = lax.ppermute(total, "seq", cores)
    direct = lax.ppermute(w_half, "head", pairs)
    matrix = shape((heads, DK, DK))
    total, level, before = call(
        merge_kernel,
        (shape((heads, DK, 2 * DK)), matrix, matrix),
        [VMEM] * 2,
        40_000_000,
        500_000,
    )(total, theirs)
    collected = [level]

    def gathered(b):
        stride = 1 << b
        groups = [[i + k * stride for k in range(4)] for i in range(seq) if (i >> b) & 3 == 0]
        return lax.all_gather(total, "seq", axis=0, axis_index_groups=groups)

    for b in range(1, outer - 2, 2):
        total, low, high, before = call(
            lambda *refs, b=b: quad_kernel(b, *refs),
            (shape((heads, DK, 2 * DK)), matrix, matrix, matrix),
            [VMEM] * 2,
            100_000_000,
            1_000_000,
        )(gathered(b), before)
        collected += [low, high]
    four = gathered(outer - 2)
    keep, give = call(
        lambda *refs: finish_kernel(outer, ring // 2, *refs),
        (shape((tokens // 2, wide)), shape((tokens // 2, wide))),
        [VMEM] * (6 + outer - 2),
        100_000_000,
        1_000_000,
        [pltpu.VMEM((tokens, wide), BF16)],
    )(core, lifted, four, before, level_weight, gate, *collected)
    give, direct = lax.optimization_barrier((give, direct))
    got = lax.ppermute(give, "head", pairs)
    across = lax.ppermute(direct, "seq", cores)
    columns = w_out.shape[1]
    step = columns // 4
    chunk = tokens // ring
    count = ring // 2
    lead = 2 * chunk
    rest = tokens // 2 - lead

    def by_columns(rows):
        return pl.BlockSpec((rows, step), lambda c: (0, c))

    whole = pl.BlockSpec((tokens // 2, wide), lambda c: (0, 0))

    def project(body, out_shape, in_specs, flops):
        return pl.pallas_call(
            body,
            grid=(columns // step,),
            out_shape=out_shape,
            in_specs=in_specs,
            out_specs=[by_columns(out.shape[0]) for out in out_shape],
            compiler_params=pltpu.CompilerParams(vmem_limit_bytes=16 << 20),
            cost_estimate=pl.CostEstimate(flops=flops, bytes_accessed=4_000_000, transcendentals=0),
        )

    first, others = project(
        project_own_kernel,
        [shape((lead, columns), F32), shape((rest, columns), F32)],
        [whole, by_columns(wide)],
        300_000_000,
    )(keep, w_out)
    ends = project(
        lambda *refs: project_kernel(0, *refs),
        [shape((chunk, columns))] * 2,
        [whole, by_columns(lead), by_columns(DK), by_columns(DK)],
        80_000_000,
    )(got, first, direct, across)
    middle = project(
        lambda *refs: project_kernel(lead, *refs),
        [shape((chunk, columns))] * (count - 2),
        [whole, by_columns(rest), by_columns(DK), by_columns(DK)],
        240_000_000,
    )(got, others, direct, across) if count > 2 else []
    terms = [ends[0], *middle, ends[1]]
    return ring_sum(terms)


def solution(mesh):
    in_specs = (
        P("seq", "head"),
        P("seq", "head"),
        P("seq", "head"),
        P("seq", "head"),
        P("head", "seq"),
        P("head", "seq"),
        P("head", None, "seq"),
        P("head", None),
    )
    out_specs = P(("seq", "head"), None)
    return jax.shard_map(
        on_device, mesh=mesh, in_specs=in_specs, out_specs=out_specs, check_vma=False
    )
```
